128 devices in a mesh: wide: 32 (over x, y, core), narrow: 4 (over z).
Axes of the slice: x: 4, y: 4, z: 4, core: 2. Of those that a mesh axis runs over, the one named last changes fastest.
Arguments:
- volume: bfloat16 [16, 2048, 512], P(None, 'wide', 'narrow'), may hold values from -24 to 24
- log_weights: float32 [6], replicated, may hold values from -2 to 2
- means: float32 [6, 48], replicated, may hold values from -2 to 2
- prec_factor: float32 [6, 48, 48], replicated, may hold values from -0.06 to 0.25, as said below
Outputs:
- responsibility: float32 [6, 16, 2048, 512], P(None, None, 'wide', 'narrow')
- new_weights: float32 [6], replicated
- new_means: float32 [6, 48], replicated
- new_cov: float32 [6, 48, 48], replicated
The draws below stay inside these ranges and needn't reach their ends.
Inputs may be any that keep to these rules, and one draw needn't show every extreme that they name: `prec_factor`: lower triangular with a positive diagonal.
All inputs are finite; a program needn't handle non-finite values.
Results may differ from the reference program's by a relative error of at most 0.00045.
The reference program's roundings to bfloat16 on the way (of `features`, `lowered` and `weighted`) count: a program that leaves them out, or rounds other values in their place, can miss the bound.
Values may be sent and summed in bfloat16 or wider, within the bound.
No kernel may reach another device: no remote copies, remote signals or barrier semaphores. Data moves between devices by JAX's collectives and lax.ppermute only.
A program may use at most 128 MiB of HBM per device.

```python
import math
import jax
import jax.numpy as jnp
from jax import lax

COMP = 6
FEAT = 48
DEPTH = 16
NX = 2048
NY = 512


def draw_volume(key, part):
    key = jax.random.fold_in(key, 5)
    row_ids = lax.broadcasted_iota(jnp.int32, (DEPTH, NX, NY), 1).astype(jnp.float32)
    position = row_ids / max(NX - 1, 1)
    row_scale = jnp.exp(position * math.log(4.0))
    values = jnp.clip(jax.random.normal(key, (DEPTH, NX, NY), jnp.float32), -6.0, 6.0)
    return (values * row_scale).astype(jnp.bfloat16)


def draw_prec_factor(key, part):
    base_key = jax.random.fold_in(key, 11)
    first_key, second_key = jax.random.split(base_key)
    diagonal_values = jax.random.uniform(first_key, (COMP, FEAT), jnp.float32, 0.1, 0.25)
    lower_values = jnp.clip(0.02 * jax.random.normal(second_key, (COMP, FEAT, FEAT), jnp.float32), -0.06, 0.06)
    row_ids = lax.broadcasted_iota(jnp.int32, (FEAT, FEAT), 0)
    col_ids = lax.broadcasted_iota(jnp.int32, (FEAT, FEAT), 1)
    strict_lower = row_ids > col_ids
    on_diagonal = row_ids == col_ids
    matrix = jnp.where(strict_lower[None], lower_values, 0.0)
    matrix = matrix + jnp.where(on_diagonal[None], diagonal_values[:, :, None], 0.0)
    return matrix


def scatter_about(own_key, extent, scale, reach, kind=jnp.bfloat16):
    return jnp.clip(scale * jax.random.normal(own_key, extent, jnp.float32), -reach, reach).astype(kind)


def setup_inputs(seed: int = 0) -> dict:
    arg_keys = jax.random.split(jax.random.key(seed), 5)
    return {
        "volume": draw_volume(jax.random.fold_in(arg_keys[4], 71), 0),
        "log_weights": jnp.clip(jax.random.uniform(arg_keys[1], (COMP,), jnp.float32, -2.0, 2.0), -2.0, 2.0),
        "means": scatter_about(arg_keys[2], (COMP, FEAT), 0.3, 2.0, jnp.float32),
        "prec_factor": draw_prec_factor(jax.random.fold_in(arg_keys[4], 71), 0),
    }


BASE_TAPS = ((1.0, 4.0, 6.0, 4.0, 1.0), (-1.0, -2.0, 0.0, 2.0, 1.0), (1.0, 0.0, -2.0, 0.0, 1.0))
TAP_NORMS = (70.0, 10.0, 6.0)
DILATIONS = (1, 2, 4, 8)
ORDER_TRIPLES = ((0, 0, 0), (0, 1, 0), (0, 0, 1), (1, 0, 0), (0, 2, 0), (0, 0, 2), (2, 0, 0), (0, 1, 1), (1, 1, 0), (1, 0, 1), (1, 1, 1), (0, 2, 2))
margin_cells = 16
block_rows = 4

def filter_axis(padded, axis_number, deriv_order, dilation, length):
    summed = None
    for tap_index in range(5):
        coefficient = BASE_TAPS[deriv_order][tap_index] / math.sqrt(TAP_NORMS[deriv_order])
        row_start = margin_cells + (tap_index - 2) * dilation
        sliced = lax.slice_in_dim(padded, row_start, row_start + length, axis=axis_number).astype(jnp.float32)
        summed = sliced * coefficient if summed is None else summed + sliced * coefficient
    return summed

def across_columns(padded, length):
    return jnp.stack([filter_axis(padded, 2, deriv_order, dilation, length) for dilation in DILATIONS for deriv_order in range(3)])

def block_features(window, block_size):
    planes = window.shape[1]
    outputs = []
    for scale_index in range(len(DILATIONS)):
        dilation = DILATIONS[scale_index]
        filtered_pairs = {}
        for triple in ORDER_TRIPLES:
            pair_key = (triple[1], triple[2])
            if pair_key not in filtered_pairs:
                filtered_pairs[pair_key] = filter_axis(window[3 * scale_index + triple[2]], 1, triple[1], dilation, block_size)
            deep_pad = jnp.pad(filtered_pairs[pair_key], ((margin_cells, margin_cells), (0, 0), (0, 0)))
            outputs.append(filter_axis(deep_pad, 0, triple[0], dilation, planes))
    stacked = jnp.stack(outputs).astype(jnp.bfloat16)
    return stacked.reshape(stacked.shape[0], -1)

def expectation(features, lowered_stack, offsets, log_prior):
    proj = jnp.dot(lowered_stack, features, preferred_element_type=jnp.float32)
    centred = proj - offsets[:, None]
    distance = lax.optimization_barrier(jnp.sum((centred * centred).reshape(log_prior.shape[0], features.shape[0], -1), axis=1))
    scores = log_prior[:, None] - 0.5 * distance
    return jax.nn.softmax(scores, axis=0)

def moments(features, resp_block):
    comp_count = resp_block.shape[0]
    feat_count = features.shape[0]
    block_counts = lax.optimization_barrier(jnp.sum(resp_block, axis=1))
    weighted = (resp_block[:, None, :] * features[None].astype(jnp.float32)).astype(jnp.bfloat16)
    weighted = weighted.reshape(comp_count * feat_count, -1)
    block_first = lax.optimization_barrier(jnp.sum(weighted.astype(jnp.float32), axis=1)).reshape(comp_count, feat_count)
    block_second = lax.dot_general(weighted, features, (((1,), (1,)), ((), ())), preferred_element_type=jnp.float32)
    return (block_counts, block_first, block_second.reshape(comp_count, feat_count, feat_count))

def parameters(log_weights, means, prec_factor):
    comp_count, feat_count = means.shape
    lowered = prec_factor.astype(jnp.bfloat16)
    lowered_stack = jnp.transpose(lowered, (0, 2, 1)).reshape(comp_count * feat_count, feat_count)
    offsets = jnp.einsum('kij,ki->kj', lowered.astype(jnp.float32), means, precision=lax.Precision.HIGHEST).reshape(-1)
    log_diag = lax.optimization_barrier(jnp.sum(jnp.log(jnp.diagonal(prec_factor, axis1=1, axis2=2)), axis=1))
    log_prior = jax.nn.log_softmax(log_weights) + log_diag - 0.5 * feat_count * math.log(2.0 * math.pi)
    return (lowered_stack, offsets, log_prior)

def finalize(counts, first, second):
    new_weights = counts / jnp.sum(counts)
    new_means = first / counts[:, None]
    new_cov = second / counts[:, None, None] - new_means[:, :, None] * new_means[:, None, :]
    return (new_weights, new_means, new_cov)

def reference(volume, log_weights, means, prec_factor):
    planes, row_count, column_count = volume.shape
    lowered_stack, offsets, log_prior = parameters(log_weights, means, prec_factor)
    padded_cols = jnp.pad(volume, ((0, 0), (0, 0), (margin_cells, margin_cells)))
    across = across_columns(padded_cols, column_count)
    rows_pad = jnp.pad(across, ((0, 0), (0, 0), (margin_cells, margin_cells), (0, 0)))

    def one_block(block_index):
        row_start = block_index * block_rows
        window = lax.dynamic_slice_in_dim(rows_pad, row_start, block_rows + 2 * margin_cells, 2)
        features = block_features(window, block_rows)
        resp_block = expectation(features, lowered_stack, offsets, log_prior)
        block_counts, block_first, block_second = moments(features, resp_block)
        return (resp_block.reshape(COMP, planes, block_rows, column_count), block_counts, block_first, block_second)
    blocks = jnp.arange(row_count // block_rows, dtype=jnp.int32)
    resp_blocks, all_counts, all_first, all_second = lax.map(one_block, blocks)
    responsibility = jnp.transpose(resp_blocks, (1, 2, 0, 3, 4)).reshape(COMP, planes, row_count, column_count)
    new_weights, new_means, new_cov = finalize(lax.optimization_barrier(jnp.sum(all_counts, axis=0)), lax.optimization_barrier(jnp.sum(all_first, axis=0)), lax.optimization_barrier(jnp.sum(all_second, axis=0)))
    return (responsibility, new_weights, new_means, new_cov)
```

```python
import math

import jax
import jax.numpy as jnp
import numpy as np
from jax import lax
from jax.experimental import pallas as pl
from jax.experimental.pallas import tpu as pltpu
from jax.sharding import PartitionSpec as P

BASE_TAPS = ((1.0, 4.0, 6.0, 4.0, 1.0), (-1.0, -2.0, 0.0, 2.0, 1.0), (1.0, 0.0, -2.0, 0.0, 1.0))
TAP_NORMS = (70.0, 10.0, 6.0)
DILATIONS = (1, 2, 4, 8)
ORDER_TRIPLES = (
    (0, 0, 0),
    (0, 1, 0),
    (0, 0, 1),
    (1, 0, 0),
    (0, 2, 0),
    (0, 0, 2),
    (2, 0, 0),
    (0, 1, 1),
    (1, 1, 0),
    (1, 0, 1),
    (1, 1, 1),
    (0, 2, 2),
)
SHIFTS = (-16, -8, -4, -2, -1, 0, 1, 2, 4, 8, 16)
MARGIN = 16
PLANES, ROWS, COLS = 16, 64, 128
COMP, FEAT = 6, 48
DEEP = 4 * FEAT + 16


def filter_matrix():
    out = np.zeros((4, PLANES, 16, 5, 5, PLANES), np.float32)
    for s, d in enumerate(DILATIONS):
        base = 4 * (s % 2)
        for j, (oz, ox, oy) in enumerate(ORDER_TRIPLES):
            plane_taps = np.outer(BASE_TAPS[ox], BASE_TAPS[oy])
            for c in range(5):
                for z in range(PLANES):
                    src = z + (c - 2) * d
                    if 0 <= src < PLANES:
                        out[s, z, base + j, :, :, src] += BASE_TAPS[oz][c] * plane_taps
    return out.reshape(4, PLANES * 16, 25 * PLANES)


def feature_scale():
    rows = [1.0 / math.sqrt(TAP_NORMS[a] * TAP_NORMS[b] * TAP_NORMS[c]) for a, b, c in ORDER_TRIPLES]
    return np.tile(np.array(rows * 4, np.float32)[:, None], (1, COLS))


def kernel(
    vol_ref, filt_ref, scale_ref, lhs_ref, prior_ref, resp_ref, sec_ref, cnt_ref, shifted, feats
):
    octet = pl.program_id(0)
    one_tile = jnp.where(lax.broadcasted_iota(jnp.int32, (16, COLS), 0) < 3, 1.0, 0.0)
    one_tile = one_tile.astype(jnp.bfloat16)

    @pl.when(octet == 0)
    def _():
        def one_row(x, carry):
            row = vol_ref[x]
            for n, shift in enumerate(SHIFTS):
                shifted[n, x] = row[:, MARGIN + shift : MARGIN + shift + COLS]
            return carry

        lax.fori_loop(0, ROWS + 2 * MARGIN, one_row, 0)
        sec_ref[...] = jnp.zeros_like(sec_ref)
        cnt_ref[...] = jnp.zeros_like(cnt_ref)

    def one_pair(pair, carry):
        x = octet * 8 + pair * 2
        blocks = []
        for s, d in enumerate(DILATIONS):
            sides = []
            for e in range(2):
                tiles = [
                    shifted[SHIFTS.index((b - 2) * d), x + e + MARGIN + (a - 2) * d]
                    for a in range(5)
                    for b in range(5)
                ]
                sides.append(jnp.concatenate(tiles, axis=0))
            rhs = jnp.concatenate(sides, axis=1)
            out = jnp.dot(filt_ref[s], rhs, preferred_element_type=jnp.float32)
            blocks.append(out.reshape(PLANES, 16, 2 * COLS))
        a, b, c, d = blocks
        rows = [a[:, :8], a[:, 8:] + b[:, :8], b[:, 8:], c[:, :8], c[:, 8:] + d[:, :8], d[:, 8:]]
        whole = jnp.concatenate(rows, axis=1)
        for e in range(2):
            part = whole[:, :, e * COLS : (e + 1) * COLS] * scale_ref[...][None]
            feats[pair * 2 + e] = part.astype(jnp.bfloat16)
        return carry

    lax.fori_loop(0, 4, one_pair, 0)

    def one_plane(z, carry):
        quads = []
        for q in range(2):
            quads.append(
                jnp.concatenate([feats[4 * q + i, z] for i in range(4)] + [one_tile], axis=0)
            )
        rhs = jnp.concatenate(quads, axis=1)
        scores = []
        for g in range(3):
            proj = jnp.dot(
                lhs_ref[g * 8 * FEAT : (g + 1) * 8 * FEAT], rhs, preferred_element_type=jnp.float32
            )
            proj = proj.reshape(FEAT, 8, 2 * COLS)
            distance = jnp.sum(proj * proj, axis=0)
            prior = prior_ref[g]
            scores.append(jnp.concatenate([prior, prior], axis=1) - 0.5 * distance)
        top = jnp.maximum(jnp.maximum(scores[0], scores[1]), scores[2])
        top = jnp.maximum(top, pltpu.roll(top, 4, 0))
        powers = [jnp.exp(s - top) for s in scores]
        total = powers[0] + powers[1] + powers[2]
        total = total + pltpu.roll(total, 4, 0)
        inverse = 1.0 / total
        for g in range(3):
            r = powers[g] * inverse
            left, right = r[:, :COLS], r[:, COLS:]
            for h in range(2):
                tile = jnp.concatenate(
                    [left[4 * h : 4 * h + 4], right[4 * h : 4 * h + 4]], axis=0
                )
                resp_ref[2 * g + h, z] = tile
                cnt_ref[2 * g + h] += tile
        features, weighted = [], []
        for i in range(8):
            f = feats[i, z]
            f32 = f.astype(jnp.float32)
            features.append(jnp.concatenate([f, one_tile], axis=0))
            weighted.append(
                jnp.concatenate(
                    [(resp_ref[k, z, i : i + 1] * f32).astype(jnp.bfloat16) for k in range(COMP)],
                    axis=0,
                )
            )
        f_all = jnp.concatenate(features, axis=1)
        w_all = jnp.concatenate(weighted, axis=1)
        sec_ref[...] += lax.dot_general(
            f_all, w_all, (((1,), (1,)), ((), ())), preferred_element_type=jnp.float32
        )
        return carry

    lax.fori_loop(0, PLANES, one_plane, 0)


def local_step(padded, lhs, prior):
    filt = jnp.asarray(filter_matrix(), jnp.bfloat16)
    scale = jnp.asarray(feature_scale())
    full = lambda *shape: pl.BlockSpec(shape, lambda o: (0,) * len(shape))
    return pl.pallas_call(
        kernel,
        grid=(ROWS // 8,),
        in_specs=[
            full(*padded.shape),
            full(*filt.shape),
            full(*scale.shape),
            full(*lhs.shape),
            full(*prior.shape),
        ],
        out_specs=[
            pl.BlockSpec((COMP, PLANES, 8, COLS), lambda o: (0, 0, o, 0)),
            full(FEAT + 16, COMP * FEAT),
            full(COMP, 8, COLS),
        ],
        out_shape=[
            jax.ShapeDtypeStruct((COMP, PLANES, ROWS, COLS), jnp.float32),
            jax.ShapeDtypeStruct((FEAT + 16, COMP * FEAT), jnp.float32),
            jax.ShapeDtypeStruct((COMP, 8, COLS), jnp.float32),
        ],
        scratch_shapes=[
            pltpu.VMEM((len(SHIFTS), ROWS + 2 * MARGIN, PLANES, COLS), jnp.bfloat16),
            pltpu.VMEM((8, PLANES, FEAT, COLS), jnp.bfloat16),
        ],
        compiler_params=pltpu.CompilerParams(
            dimension_semantics=("arbitrary",), vmem_limit_bytes=50 * 2**20
        ),
        name="mixture_step",
    )(padded, filt, scale, lhs, prior)


def parameters(log_weights, means, prec_factor):
    lowered = prec_factor.astype(jnp.bfloat16)
    offsets = jnp.einsum(
        "kij,ki->kj", lowered.astype(jnp.float32), means, precision=lax.Precision.HIGHEST
    )
    log_diag = jnp.sum(jnp.log(jnp.diagonal(prec_factor, axis1=1, axis2=2)), axis=1)
    log_prior = jax.nn.log_softmax(log_weights) + log_diag - 0.5 * FEAT * math.log(2.0 * math.pi)
    columns = jnp.transpose(lowered.reshape(3, 2, FEAT, FEAT), (0, 3, 1, 2))
    eye = jnp.eye(4, dtype=jnp.bfloat16)
    stacked = columns[:, :, :, None, None, :] * eye[None, None, None, :, :, None]
    stacked = stacked.reshape(COMP * FEAT * 4, 4 * FEAT)
    rest = -jnp.transpose(offsets.reshape(3, 2, FEAT), (0, 2, 1))
    terms = []
    for _ in range(3):
        term = lax.reduce_precision(rest, 8, 7)
        terms.append(term)
        rest = rest - term
    tail = jnp.stack(terms + [jnp.zeros_like(rest)] * 13, axis=-1).astype(jnp.bfloat16)
    tail = jnp.broadcast_to(tail[:, :, :, None, :], (3, FEAT, 2, 4, 16)).reshape(-1, 16)
    lhs = jnp.concatenate([stacked, tail], axis=1)
    prior = jnp.broadcast_to(log_prior.reshape(3, 2, 1, 1), (3, 2, 4, COLS)).reshape(3, 8, COLS)
    return lhs, prior


def padded_2(cells, axis, dim, width):
    count = lax.axis_size(axis)
    ends = count - 1
    head = lax.slice_in_dim(cells, 0, width, axis=dim)
    tail = lax.slice_in_dim(cells, cells.shape[dim] - width, cells.shape[dim], axis=dim)
    before = lax.ppermute(tail, axis, [(i, i + 1) for i in range(ends)])
    after = lax.ppermute(head, axis, [(i + 1, i) for i in range(ends)])
    return jnp.concatenate([before, cells, after], axis=dim)


def wide_perm(move):
    perm = []
    for i in range(32):
        x, y, c = move(i // 8, (i // 2) % 4, i % 2)
        perm.append((i, (x * 4 + y) * 2 + c))
    return perm


def device_sum(part):
    part = part + lax.ppermute(part, "wide", wide_perm(lambda x, y, c: (x, y, 1 - c)))
    narrow = [
        lax.ppermute(part, "narrow", [(i, (i + d) % 4) for i in range(4)]) for d in (1, 2, 3)
    ]
    part = ((part + narrow[0]) + (narrow[1] + narrow[2]))
    for axis in range(2):
        got = []
        for d in (1, 2, 3):
            if axis == 0:
                perm = wide_perm(lambda x, y, c: (x, (y + d) % 4, c))
            else:
                perm = wide_perm(lambda x, y, c: ((x + d) % 4, y, c))
            got.append(lax.ppermute(part, "wide", perm))
        part = (part + got[0]) + (got[1] + got[2])
    return part


def shards(volume, log_weights, means, prec_factor):
    lhs, prior = parameters(log_weights, means, prec_factor)
    cells = padded_2(volume, "narrow", 2, MARGIN)
    cells = padded_2(cells, "wide", 1, MARGIN)
    cells = jnp.transpose(cells, (1, 0, 2))
    cells = jnp.pad(cells, ((0, 0), (0, 0), (0, 96)))
    responsibility, sec, cnt = local_step(cells, lhs, prior)
    counts = jnp.sum(cnt, axis=(1, 2))
    flat = jnp.concatenate([sec[: FEAT + 1].reshape(-1), counts, jnp.zeros((218,), jnp.float32)])
    flat = device_sum(flat.reshape(112, 128)).reshape(-1)
    size = FEAT * COMP * FEAT
    second = jnp.transpose(flat[:size].reshape(FEAT, COMP, FEAT), (1, 2, 0))
    first = flat[size : size + COMP * FEAT].reshape(COMP, FEAT)
    counts = flat[size + COMP * FEAT : size + COMP * FEAT + COMP]
    new_weights = counts / jnp.sum(counts)
    new_means = first / counts[:, None]
    new_cov = second / counts[:, None, None] - new_means[:, :, None] * new_means[:, None, :]
    return (responsibility, new_weights, new_means, new_cov)


def solution(mesh):
    in_specs = (P(None, "wide", "narrow"), P(), P(), P())
    out_specs = (P(None, None, "wide", "narrow"), P(), P(), P())
    return jax.shard_map(shards, mesh=mesh, in_specs=in_specs, out_specs=out_specs, check_vma=False)
```

```python
import math

import jax
import jax.numpy as jnp
import numpy as np
from jax import lax
from jax.experimental import pallas as pl
from jax.experimental.pallas import tpu as pltpu
from jax.sharding import PartitionSpec as P

BASE_TAPS = ((1.0, 4.0, 6.0, 4.0, 1.0), (-1.0, -2.0, 0.0, 2.0, 1.0), (1.0, 0.0, -2.0, 0.0, 1.0))
TAP_NORMS = (70.0, 10.0, 6.0)
DILATIONS = (1, 2, 4, 8)
ORDER_TRIPLES = (
    (0, 0, 0),
    (0, 1, 0),
    (0, 0, 1),
    (1, 0, 0),
    (0, 2, 0),
    (0, 0, 2),
    (2, 0, 0),
    (0, 1, 1),
    (1, 1, 0),
    (1, 0, 1),
    (1, 1, 1),
    (0, 2, 2),
)
SHIFTS = (-16, -8, -4, -2, -1, 0, 1, 2, 4, 8, 16)
MARGIN = 16
PLANES, ROWS, COLS = 16, 64, 128
COMP, FEAT = 6, 48
DEEP = 4 * FEAT + 16


def filter_matrix():
    out = np.zeros((4, PLANES, 16, 5, 5, PLANES), np.float32)
    for s, d in enumerate(DILATIONS):
        base = 4 * (s % 2)
        for j, (oz, ox, oy) in enumerate(ORDER_TRIPLES):
            plane_taps = np.outer(BASE_TAPS[ox], BASE_TAPS[oy])
            for c in range(5):
                for z in range(PLANES):
                    src = z + (c - 2) * d
                    if 0 <= src < PLANES:
                        out[s, z, base + j, :, :, src] += BASE_TAPS[oz][c] * plane_taps
    return out.reshape(4, PLANES * 16, 25 * PLANES)


def feature_scale():
    rows = [1.0 / math.sqrt(TAP_NORMS[a] * TAP_NORMS[b] * TAP_NORMS[c]) for a, b, c in ORDER_TRIPLES]
    return np.tile(np.array(rows * 4, np.float32)[:, None], (1, COLS))


def interleave_matrix():
    out = np.zeros((FEAT, 8, 8, FEAT), np.float32)
    for j in range(FEAT):
        for c in range(8):
            out[j, c, c, j] = 1.0
    return out.reshape(8 * FEAT, 8 * FEAT)


def kernel(
    vol_ref,
    filt_ref,
    scale_ref,
    lhs_ref,
    prior_ref,
    resp_ref,
    moment_ref,
    shifted,
    feats,
    sec_ref,
    cnt_ref,
):
    octet = pl.program_id(0)
    one_tile = jnp.where(lax.broadcasted_iota(jnp.int32, (16, COLS), 0) < 3, 1.0, 0.0)
    one_tile = one_tile.astype(jnp.bfloat16)

    @pl.when(octet == 0)
    def _():
        def one_row(x, carry):
            row = vol_ref[x]
            for n, shift in enumerate(SHIFTS):
                shifted[n, x] = row[:, MARGIN + shift : MARGIN + shift + COLS]
            return carry

        lax.fori_loop(0, ROWS + 2 * MARGIN, one_row, 0, unroll=16)
        sec_ref[...] = jnp.zeros_like(sec_ref)
        cnt_ref[...] = jnp.zeros_like(cnt_ref)

    def one_pair(pair, carry):
        x = octet * 8 + pair * 2
        blocks = []
        for s, d in enumerate(DILATIONS):
            sides = []
            for e in range(2):
                tiles = [
                    shifted[SHIFTS.index((b - 2) * d), x + e + MARGIN + (a - 2) * d]
                    for a in range(5)
                    for b in range(5)
                ]
                sides.append(jnp.concatenate(tiles, axis=0))
            rhs = jnp.concatenate(sides, axis=1)
            out = jnp.dot(filt_ref[s], rhs, preferred_element_type=jnp.float32)
            blocks.append(out.reshape(PLANES, 16, 2 * COLS))
        a, b, c, d = blocks
        rows = [a[:, :8], a[:, 8:] + b[:, :8], b[:, 8:], c[:, :8], c[:, 8:] + d[:, :8], d[:, 8:]]
        whole = jnp.concatenate(rows, axis=1)
        for e in range(2):
            part = whole[:, :, e * COLS : (e + 1) * COLS] * scale_ref[...][None]
            feats[pair * 2 + e] = part.astype(jnp.bfloat16)
        return carry

    lax.fori_loop(0, 4, one_pair, 0, unroll=4)

    def expect(z):
        quads = []
        for q in range(2):
            quads.append(
                jnp.concatenate([feats[4 * q + i, z] for i in range(4)] + [one_tile], axis=0)
            )
        rhs = jnp.concatenate(quads, axis=1)
        scores = []
        for g in range(3):
            proj = jnp.dot(
                lhs_ref[g * 8 * FEAT : (g + 1) * 8 * FEAT], rhs, preferred_element_type=jnp.float32
            )
            proj = proj.reshape(FEAT, 8, 2 * COLS)
            distance = jnp.sum(proj * proj, axis=0)
            prior = prior_ref[g]
            scores.append(jnp.concatenate([prior, prior], axis=1) - 0.5 * distance)
        top = jnp.maximum(jnp.maximum(scores[0], scores[1]), scores[2])
        top = jnp.maximum(top, pltpu.roll(top, 4, 0))
        powers = [jnp.exp(s - top) for s in scores]
        total = powers[0] + powers[1] + powers[2]
        total = total + pltpu.roll(total, 4, 0)
        inverse = 1.0 / total
        for g in range(3):
            r = powers[g] * inverse
            left, right = r[:, :COLS], r[:, COLS:]
            for h in range(2):
                tile = jnp.concatenate(
                    [left[4 * h : 4 * h + 4], right[4 * h : 4 * h + 4]], axis=0
                )
                resp_ref[2 * g + h, z] = tile
                cnt_ref[2 * g + h] += tile

    def moment(z):
        features, weighted = [], []
        tiles = [resp_ref[k, z] for k in range(COMP)]
        for i in range(8):
            f = feats[i, z]
            f32 = f.astype(jnp.float32)
            features.append(jnp.concatenate([f, one_tile], axis=0))
            weighted.append(
                jnp.concatenate(
                    [(tiles[k][i : i + 1] * f32).astype(jnp.bfloat16) for k in range(COMP)],
                    axis=0,
                )
            )
        f_all = jnp.concatenate(features, axis=1)
        w_all = jnp.concatenate(weighted, axis=1)
        sec_ref[...] += lax.dot_general(
            w_all, f_all, (((1,), (1,)), ((), ())), preferred_element_type=jnp.float32
        )

    def expect_step(z, carry):
        expect(z)
        return carry

    def moment_step(z, carry):
        moment(z)
        return carry

    lax.fori_loop(0, PLANES, expect_step, 0, unroll=16)
    lax.fori_loop(0, PLANES, moment_step, 0, unroll=16)

    @pl.when(octet == pl.num_programs(0) - 1)
    def _():
        lane = lax.broadcasted_iota(jnp.int32, (FEAT, 128), 1)
        for m in range(3):
            first, second = [sec_ref[k * FEAT : (k + 1) * FEAT] for k in (2 * m, 2 * m + 1)]
            both = jnp.concatenate([first, second], axis=1)
            both = jnp.where(lane == FEAT + 1, jnp.sum(cnt_ref[2 * m]), both)
            both = jnp.where(lane == 64 + FEAT + 1, jnp.sum(cnt_ref[2 * m + 1]), both)
            moment_ref[m * FEAT : (m + 1) * FEAT] = both


def prepare_kernel(weight_ref, mean_ref, factor_ref, order_ref, lhs_ref, prior_ref):
    logits = weight_ref[...]
    top = jnp.max(logits, axis=1, keepdims=True)
    log_total = jnp.log(jnp.sum(jnp.exp(logits - top), axis=1, keepdims=True)) + top
    on_diagonal = lax.broadcasted_iota(jnp.int32, (FEAT, FEAT), 0) == lax.broadcasted_iota(
        jnp.int32, (FEAT, FEAT), 1
    )
    lane = lax.broadcasted_iota(jnp.int32, (FEAT, 256), 1)
    half = lax.broadcasted_iota(jnp.int32, (8, COLS), 0) < 4
    order = order_ref[...]
    for g in range(3):
        rows, priors = [], []
        for h in range(2):
            k = 2 * g + h
            factor = factor_ref[k]
            log_diag = jnp.sum(jnp.where(on_diagonal, jnp.log(jnp.where(on_diagonal, factor, 1.0)), 0.0))
            prior = logits[:, k : k + 1] - log_total + log_diag - 0.5 * FEAT * math.log(2.0 * math.pi)
            priors.append(jnp.broadcast_to(prior, (8, COLS)))
            columns = factor.astype(jnp.bfloat16).astype(jnp.float32).T
            offset = jnp.sum(columns * mean_ref[k : k + 1], axis=1, keepdims=True)
            rest = -offset
            tail = jnp.zeros((FEAT, 256), jnp.float32)
            for t in range(3):
                term = rest.astype(jnp.bfloat16).astype(jnp.float32)
                tail = jnp.where(lane == 4 * FEAT + t, term, tail)
                rest = rest - term
            wide = jnp.concatenate([columns, jnp.zeros((FEAT, 256 - FEAT), jnp.float32)], axis=1)
            for x in range(4):
                moved = wide if x == 0 else pltpu.roll(wide, x * FEAT, 1)
                rows.append((moved + tail).astype(jnp.bfloat16))
        block = jnp.dot(order, jnp.concatenate(rows, axis=0), preferred_element_type=jnp.float32)
        lhs_ref[g * 8 * FEAT : (g + 1) * 8 * FEAT] = block[:, :DEEP].astype(jnp.bfloat16)
        prior_ref[g] = jnp.where(half, priors[0], priors[1])


def vmem_specs(count):
    return [pl.BlockSpec(memory_space=pltpu.VMEM)] * count


def prepare(log_weights, means, prec_factor):
    order = jnp.asarray(interleave_matrix(), jnp.bfloat16)
    return pl.pallas_call(
        prepare_kernel,
        in_specs=vmem_specs(4),
        out_specs=vmem_specs(2),
        out_shape=[
            jax.ShapeDtypeStruct((COMP * FEAT * 4, DEEP), jnp.bfloat16),
            jax.ShapeDtypeStruct((3, 8, COLS), jnp.float32),
        ],
        cost_estimate=pl.CostEstimate(flops=10**8, bytes_accessed=2 * 10**6, transcendentals=2 * 10**4),
        name="prepare",
    )(log_weights.reshape(1, COMP), means, prec_factor, order)


def finish_kernel(moment_ref, weight_ref, mean_ref, cov_ref):
    on_diagonal = lax.broadcasted_iota(jnp.int32, (FEAT, FEAT), 0) == lax.broadcasted_iota(
        jnp.int32, (FEAT, FEAT), 1
    )
    lane = lax.broadcasted_iota(jnp.int32, (1, COMP), 1)
    counts = jnp.zeros((1, COMP), jnp.float32)
    for k in range(COMP):
        both = moment_ref[k // 2 * FEAT : (k // 2 + 1) * FEAT]
        block = both[:, k % 2 * 64 : k % 2 * 64 + 64]
        count = block[:1, FEAT + 1 : FEAT + 2]
        column = block[:, FEAT : FEAT + 1] / count
        row = jnp.sum(jnp.where(on_diagonal, column, 0.0), axis=0, keepdims=True)
        cov_ref[k] = block[:, :FEAT] / count - column * row
        mean_ref[k : k + 1] = row
        counts = jnp.where(lane == k, count, counts)
    weight_ref[...] = counts / jnp.sum(counts, axis=1, keepdims=True)


def finish(moments):
    new_weights, new_means, new_cov = pl.pallas_call(
        finish_kernel,
        in_specs=vmem_specs(1),
        out_specs=vmem_specs(3),
        out_shape=[
            jax.ShapeDtypeStruct((1, COMP), jnp.float32),
            jax.ShapeDtypeStruct((COMP, FEAT), jnp.float32),
            jax.ShapeDtypeStruct((COMP, FEAT, FEAT), jnp.float32),
        ],
        name="finish",
    )(moments)
    return new_weights.reshape(COMP), new_means, new_cov


def local_step(padded, lhs, prior):
    filt = jnp.asarray(filter_matrix(), jnp.bfloat16)
    scale = jnp.asarray(feature_scale())
    full = lambda *shape: pl.BlockSpec(shape, lambda o: (0,) * len(shape))
    return pl.pallas_call(
        kernel,
        grid=(ROWS // 8,),
        in_specs=[
            full(*padded.shape),
            full(*filt.shape),
            full(*scale.shape),
            full(*lhs.shape),
            full(*prior.shape),
        ],
        out_specs=[
            pl.BlockSpec((COMP, PLANES, 8, COLS), lambda o: (0, 0, o, 0)),
            full(3 * FEAT, 128),
        ],
        out_shape=[
            jax.ShapeDtypeStruct((COMP, PLANES, ROWS, COLS), jnp.float32),
            jax.ShapeDtypeStruct((3 * FEAT, 128), jnp.float32),
        ],
        scratch_shapes=[
            pltpu.VMEM((len(SHIFTS), ROWS + 2 * MARGIN, PLANES, COLS), jnp.bfloat16),
            pltpu.VMEM((8, PLANES, FEAT, COLS), jnp.bfloat16),
            pltpu.VMEM((COMP * FEAT, FEAT + 16), jnp.float32),
            pltpu.VMEM((COMP, 8, COLS), jnp.float32),
        ],
        compiler_params=pltpu.CompilerParams(
            dimension_semantics=("arbitrary",), vmem_limit_bytes=50 * 2**20
        ),
        name="mixture_step",
    )(padded, filt, scale, lhs, prior)


def padded_2(cells, axis, dim, width):
    count = lax.axis_size(axis)
    ends = count - 1
    head = lax.slice_in_dim(cells, 0, width, axis=dim)
    tail = lax.slice_in_dim(cells, cells.shape[dim] - width, cells.shape[dim], axis=dim)
    before = lax.ppermute(tail, axis, [(i, i + 1) for i in range(ends)])
    after = lax.ppermute(head, axis, [(i + 1, i) for i in range(ends)])
    return jnp.concatenate([before, cells, after], axis=dim)


def wide_perm(move):
    perm = []
    for i in range(32):
        x, y, c = move(i // 8, (i // 2) % 4, i % 2)
        perm.append((i, (x * 4 + y) * 2 + c))
    return perm


def device_sum(part):
    part = part + lax.ppermute(part, "wide", wide_perm(lambda x, y, c: (x, y, 1 - c)))
    narrow = [
        lax.ppermute(part, "narrow", [(i, (i + d) % 4) for i in range(4)]) for d in (1, 2, 3)
    ]
    part = ((part + narrow[0]) + (narrow[1] + narrow[2]))
    for axis in range(2):
        got = []
        for d in (1, 2, 3):
            if axis == 0:
                perm = wide_perm(lambda x, y, c: (x, (y + d) % 4, c))
            else:
                perm = wide_perm(lambda x, y, c: ((x + d) % 4, y, c))
            got.append(lax.ppermute(part, "wide", perm))
        part = (part + got[0]) + (got[1] + got[2])
    return part


def shards(volume, log_weights, means, prec_factor):
    lhs, prior = prepare(log_weights, means, prec_factor)
    cells = padded_2(volume, "narrow", 2, MARGIN)
    cells = padded_2(cells, "wide", 1, MARGIN)
    responsibility, moments = local_step(jnp.transpose(cells, (1, 0, 2)), lhs, prior)
    return (responsibility,) + finish(device_sum(moments))


def solution(mesh):
    in_specs = (P(None, "wide", "narrow"), P(), P(), P())
    out_specs = (P(None, None, "wide", "narrow"), P(), P(), P())
    return jax.shard_map(shards, mesh=mesh, in_specs=in_specs, out_specs=out_specs, check_vma=False)
```

```python
import math

import jax
import jax.numpy as jnp
import numpy as np
from jax import lax
from jax.experimental import pallas as pl
from jax.experimental.pallas import tpu as pltpu
from jax.sharding import PartitionSpec as P

BASE_TAPS = ((1.0, 4.0, 6.0, 4.0, 1.0), (-1.0, -2.0, 0.0, 2.0, 1.0), (1.0, 0.0, -2.0, 0.0, 1.0))
TAP_NORMS = (70.0, 10.0, 6.0)
DILATIONS = (1, 2, 4, 8)
ORDER_TRIPLES = (
    (0, 0, 0),
    (0, 1, 0),
    (0, 0, 1),
    (1, 0, 0),
    (0, 2, 0),
    (0, 0, 2),
    (2, 0, 0),
    (0, 1, 1),
    (1, 1, 0),
    (1, 0, 1),
    (1, 1, 1),
    (0, 2, 2),
)
SHIFTS = (-16, -8, -4, -2, -1, 0, 1, 2, 4, 8, 16)
MARGIN = 16
PLANES, ROWS, COLS = 16, 64, 128
COMP, FEAT = 6, 48
DEEP = 4 * FEAT + 16


def filter_matrix():
    out = np.zeros((4, PLANES, 16, 5, 5, PLANES), np.float32)
    for s, d in enumerate(DILATIONS):
        base = 4 * (s % 2)
        for j, (oz, ox, oy) in enumerate(ORDER_TRIPLES):
            plane_taps = np.outer(BASE_TAPS[ox], BASE_TAPS[oy])
            for c in range(5):
                for z in range(PLANES):
                    src = z + (c - 2) * d
                    if 0 <= src < PLANES:
                        out[s, z, base + j, :, :, src] += BASE_TAPS[oz][c] * plane_taps
    return out.reshape(4, PLANES * 16, 25 * PLANES)


def feature_scale():
    rows = [1.0 / math.sqrt(TAP_NORMS[a] * TAP_NORMS[b] * TAP_NORMS[c]) for a, b, c in ORDER_TRIPLES]
    return np.tile(np.array(rows * 4, np.float32)[:, None], (1, COLS))


def interleave_matrix():
    out = np.zeros((FEAT, 8, 8, FEAT), np.float32)
    for j in range(FEAT):
        for c in range(8):
            out[j, c, c, j] = 1.0
    return out.reshape(8 * FEAT, 8 * FEAT)


def kernel(
    before_ref,
    rows_ref,
    after_ref,
    left_ref,
    right_ref,
    filt_ref,
    scale_ref,
    lhs_ref,
    prior_ref,
    resp_ref,
    moment_ref,
    shifted,
    feats,
    sec_ref,
    cnt_ref,
):
    octet = pl.program_id(0)
    one_tile = jnp.where(lax.broadcasted_iota(jnp.int32, (16, COLS), 0) < 3, 1.0, 0.0)
    one_tile = one_tile.astype(jnp.bfloat16)

    @pl.when(octet == 0)
    def _():
        def fill(x, get_row, left, right):
            for m in range(8):
                row = get_row(m)
                for n, shift in enumerate(SHIFTS):
                    if shift < 0:
                        edge = left[:, 16 * m + 16 + shift : 16 * m + 16]
                        moved = jnp.concatenate([edge, row[:, : COLS + shift]], axis=1)
                    elif shift > 0:
                        edge = right[:, 16 * m : 16 * m + shift]
                        moved = jnp.concatenate([row[:, shift:], edge], axis=1)
                    else:
                        moved = row
                    shifted[n, x + m] = moved

        for g in range(2):
            get_before = lambda m: before_ref[8 * g + m]
            get_after = lambda m: after_ref[8 * g + m]
            fill(8 * g, get_before, before_ref[16 + g], before_ref[18 + g])
            fill(MARGIN + ROWS + 8 * g, get_after, after_ref[16 + g], after_ref[18 + g])

        def one_group(g, carry):
            fill(MARGIN + 8 * g, lambda m: rows_ref[8 * g + m], left_ref[g], right_ref[g])
            return carry

        lax.fori_loop(0, ROWS // 8, one_group, 0, unroll=2)
        sec_ref[...] = jnp.zeros_like(sec_ref)
        cnt_ref[...] = jnp.zeros_like(cnt_ref)

    def one_pair(pair, carry):
        x = octet * 8 + pair * 2
        blocks = []
        for s, d in enumerate(DILATIONS):
            sides = []
            for e in range(2):
                tiles = [
                    shifted[SHIFTS.index((b - 2) * d), x + e + MARGIN + (a - 2) * d]
                    for a in range(5)
                    for b in range(5)
                ]
                sides.append(jnp.concatenate(tiles, axis=0))
            rhs = jnp.concatenate(sides, axis=1)
            out = jnp.dot(filt_ref[s], rhs, preferred_element_type=jnp.float32)
            blocks.append(out.reshape(PLANES, 16, 2 * COLS))
        a, b, c, d = blocks
        rows = [a[:, :8], a[:, 8:] + b[:, :8], b[:, 8:], c[:, :8], c[:, 8:] + d[:, :8], d[:, 8:]]
        whole = jnp.concatenate(rows, axis=1)
        for e in range(2):
            part = whole[:, :, e * COLS : (e + 1) * COLS] * scale_ref[...][None]
            feats[pair * 2 + e] = part.astype(jnp.bfloat16)
        return carry

    lax.fori_loop(0, 4, one_pair, 0, unroll=4)

    def expect(z):
        quads = []
        for q in range(2):
            quads.append(
                jnp.concatenate([feats[4 * q + i, z] for i in range(4)] + [one_tile], axis=0)
            )
        rhs = jnp.concatenate(quads, axis=1)
        scores = []
        for g in range(3):
            proj = jnp.dot(
                lhs_ref[g * 8 * FEAT : (g + 1) * 8 * FEAT], rhs, preferred_element_type=jnp.float32
            )
            proj = proj.reshape(FEAT, 8, 2 * COLS)
            distance = jnp.sum(proj * proj, axis=0)
            prior = prior_ref[g]
            scores.append(jnp.concatenate([prior, prior], axis=1) - 0.5 * distance)
        top = jnp.maximum(jnp.maximum(scores[0], scores[1]), scores[2])
        top = jnp.maximum(top, pltpu.roll(top, 4, 0))
        powers = [jnp.exp(s - top) for s in scores]
        total = powers[0] + powers[1] + powers[2]
        total = total + pltpu.roll(total, 4, 0)
        inverse = 1.0 / total
        for g in range(3):
            r = powers[g] * inverse
            left, right = r[:, :COLS], r[:, COLS:]
            for h in range(2):
                tile = jnp.concatenate(
                    [left[4 * h : 4 * h + 4], right[4 * h : 4 * h + 4]], axis=0
                )
                resp_ref[2 * g + h, z] = tile
                cnt_ref[2 * g + h] += tile

    def moment(z):
        features, weighted = [], []
        tiles = [resp_ref[k, z] for k in range(COMP)]
        for i in range(8):
            f = feats[i, z]
            f32 = f.astype(jnp.float32)
            features.append(jnp.concatenate([f, one_tile], axis=0))
            weighted.append(
                jnp.concatenate(
                    [(tiles[k][i : i + 1] * f32).astype(jnp.bfloat16) for k in range(COMP)],
                    axis=0,
                )
            )
        f_all = jnp.concatenate(features, axis=1)
        w_all = jnp.concatenate(weighted, axis=1)
        sec_ref[...] += lax.dot_general(
            w_all, f_all, (((1,), (1,)), ((), ())), preferred_element_type=jnp.float32
        )

    def expect_step(z, carry):
        expect(z)
        return carry

    def moment_step(z, carry):
        moment(z)
        return carry

    lax.fori_loop(0, PLANES, expect_step, 0, unroll=16)
    lax.fori_loop(0, PLANES, moment_step, 0, unroll=16)

    @pl.when(octet == pl.num_programs(0) - 1)
    def _():
        lane = lax.broadcasted_iota(jnp.int32, (FEAT, 128), 1)
        for m in range(3):
            first, second = [sec_ref[k * FEAT : (k + 1) * FEAT] for k in (2 * m, 2 * m + 1)]
            both = jnp.concatenate([first, second], axis=1)
            both = jnp.where(lane == FEAT + 1, jnp.sum(cnt_ref[2 * m]), both)
            both = jnp.where(lane == 64 + FEAT + 1, jnp.sum(cnt_ref[2 * m + 1]), both)
            moment_ref[m * FEAT : (m + 1) * FEAT] = both


def prepare_kernel(weight_ref, mean_ref, factor_ref, order_ref, lhs_ref, prior_ref):
    logits = weight_ref[...]
    top = jnp.max(logits, axis=1, keepdims=True)
    log_total = jnp.log(jnp.sum(jnp.exp(logits - top), axis=1, keepdims=True)) + top
    on_diagonal = lax.broadcasted_iota(jnp.int32, (FEAT, FEAT), 0) == lax.broadcasted_iota(
        jnp.int32, (FEAT, FEAT), 1
    )
    lane = lax.broadcasted_iota(jnp.int32, (FEAT, 256), 1)
    half = lax.broadcasted_iota(jnp.int32, (8, COLS), 0) < 4
    order = order_ref[...]
    for g in range(3):
        rows, priors = [], []
        for h in range(2):
            k = 2 * g + h
            factor = factor_ref[k]
            log_diag = jnp.sum(jnp.where(on_diagonal, jnp.log(jnp.where(on_diagonal, factor, 1.0)), 0.0))
            prior = logits[:, k : k + 1] - log_total + log_diag - 0.5 * FEAT * math.log(2.0 * math.pi)
            priors.append(jnp.broadcast_to(prior, (8, COLS)))
            columns = factor.astype(jnp.bfloat16).astype(jnp.float32).T
            offset = jnp.sum(columns * mean_ref[k : k + 1], axis=1, keepdims=True)
            rest = -offset
            tail = jnp.zeros((FEAT, 256), jnp.float32)
            for t in range(3):
                term = rest.astype(jnp.bfloat16).astype(jnp.float32)
                tail = jnp.where(lane == 4 * FEAT + t, term, tail)
                rest = rest - term
            wide = jnp.concatenate([columns, jnp.zeros((FEAT, 256 - FEAT), jnp.float32)], axis=1)
            for x in range(4):
                moved = wide if x == 0 else pltpu.roll(wide, x * FEAT, 1)
                rows.append((moved + tail).astype(jnp.bfloat16))
        block = jnp.dot(order, jnp.concatenate(rows, axis=0), preferred_element_type=jnp.float32)
        lhs_ref[g * 8 * FEAT : (g + 1) * 8 * FEAT] = block[:, :DEEP].astype(jnp.bfloat16)
        prior_ref[g] = jnp.where(half, priors[0], priors[1])


def vmem_specs(count):
    return [pl.BlockSpec(memory_space=pltpu.VMEM)] * count


def prepare(log_weights, means, prec_factor):
    order = jnp.asarray(interleave_matrix(), jnp.bfloat16)
    return pl.pallas_call(
        prepare_kernel,
        in_specs=vmem_specs(4),
        out_specs=vmem_specs(2),
        out_shape=[
            jax.ShapeDtypeStruct((COMP * FEAT * 4, DEEP), jnp.bfloat16),
            jax.ShapeDtypeStruct((3, 8, COLS), jnp.float32),
        ],
        cost_estimate=pl.CostEstimate(flops=10**8, bytes_accessed=2 * 10**6, transcendentals=2 * 10**4),
        name="prepare",
    )(log_weights.reshape(1, COMP), means, prec_factor, order)


def finish_kernel(a_ref, b_ref, c_ref, d_ref, weight_ref, mean_ref, cov_ref):
    on_diagonal = lax.broadcasted_iota(jnp.int32, (FEAT, FEAT), 0) == lax.broadcasted_iota(
        jnp.int32, (FEAT, FEAT), 1
    )
    lane = lax.broadcasted_iota(jnp.int32, (1, COMP), 1)
    counts = jnp.zeros((1, COMP), jnp.float32)
    for k in range(COMP):
        at = slice(k // 2 * FEAT, (k // 2 + 1) * FEAT)
        both = (a_ref[at] + b_ref[at]) + (c_ref[at] + d_ref[at])
        block = both[:, k % 2 * 64 : k % 2 * 64 + 64]
        count = block[:1, FEAT + 1 : FEAT + 2]
        column = block[:, FEAT : FEAT + 1] / count
        row = jnp.sum(jnp.where(on_diagonal, column, 0.0), axis=0, keepdims=True)
        cov_ref[k] = block[:, :FEAT] / count - column * row
        mean_ref[k : k + 1] = row
        counts = jnp.where(lane == k, count, counts)
    weight_ref[...] = counts / jnp.sum(counts, axis=1, keepdims=True)


def finish(*parts):
    new_weights, new_means, new_cov = pl.pallas_call(
        finish_kernel,
        in_specs=vmem_specs(4),
        out_specs=vmem_specs(3),
        out_shape=[
            jax.ShapeDtypeStruct((1, COMP), jnp.float32),
            jax.ShapeDtypeStruct((COMP, FEAT), jnp.float32),
            jax.ShapeDtypeStruct((COMP, FEAT, FEAT), jnp.float32),
        ],
        name="finish",
    )(*parts)
    return new_weights.reshape(COMP), new_means, new_cov


def local_step(pieces, lhs, prior):
    filt = jnp.asarray(filter_matrix(), jnp.bfloat16)
    scale = jnp.asarray(feature_scale())
    full = lambda *shape: pl.BlockSpec(shape, lambda o: (0,) * len(shape))
    return pl.pallas_call(
        kernel,
        grid=(ROWS // 8,),
        in_specs=[
            *[full(*piece.shape) for piece in pieces],
            full(*filt.shape),
            full(*scale.shape),
            full(*lhs.shape),
            full(*prior.shape),
        ],
        out_specs=[
            pl.BlockSpec((COMP, PLANES, 8, COLS), lambda o: (0, 0, o, 0)),
            full(3 * FEAT, 128),
        ],
        out_shape=[
            jax.ShapeDtypeStruct((COMP, PLANES, ROWS, COLS), jnp.float32),
            jax.ShapeDtypeStruct((3 * FEAT, 128), jnp.float32),
        ],
        scratch_shapes=[
            pltpu.VMEM((len(SHIFTS), ROWS + 2 * MARGIN, PLANES, COLS), jnp.bfloat16),
            pltpu.VMEM((8, PLANES, FEAT, COLS), jnp.bfloat16),
            pltpu.VMEM((COMP * FEAT, FEAT + 16), jnp.float32),
            pltpu.VMEM((COMP, 8, COLS), jnp.float32),
        ],
        compiler_params=pltpu.CompilerParams(
            dimension_semantics=("arbitrary",), vmem_limit_bytes=50 * 2**20
        ),
        name="mixture_step",
    )(*pieces, filt, scale, lhs, prior)


def pack_kernel(rows_ref, head_ref, tail_ref):
    for n in range(ROWS // 8):
        group = [rows_ref[8 * n + m] for m in range(8)]
        head_ref[n] = jnp.concatenate([row[:, :MARGIN] for row in group], axis=1)
        tail_ref[n] = jnp.concatenate([row[:, COLS - MARGIN :] for row in group], axis=1)


def pack(rows):
    shape = jax.ShapeDtypeStruct((ROWS // 8, PLANES, COLS), jnp.bfloat16)
    return pl.pallas_call(
        pack_kernel,
        in_specs=vmem_specs(1),
        out_specs=vmem_specs(2),
        out_shape=[shape, shape],
        name="pack",
    )(rows)


def neighbours(to_next, to_previous, axis):
    ends = lax.axis_size(axis) - 1
    before = lax.ppermute(to_next, axis, [(i, i + 1) for i in range(ends)])
    after = lax.ppermute(to_previous, axis, [(i + 1, i) for i in range(ends)])
    return before, after


def wide_perm(move):
    perm = []
    for i in range(32):
        x, y, c = move(i // 8, (i // 2) % 4, i % 2)
        perm.append((i, (x * 4 + y) * 2 + c))
    return perm


def device_sum(part):
    part = part + lax.ppermute(part, "wide", wide_perm(lambda x, y, c: (x, y, 1 - c)))
    narrow = [
        lax.ppermute(part, "narrow", [(i, (i + d) % 4) for i in range(4)]) for d in (1, 2, 3)
    ]
    part = ((part + narrow[0]) + (narrow[1] + narrow[2]))
    for axis in range(2):
        got = []
        for d in (1, 2, 3):
            if axis == 0:
                perm = wide_perm(lambda x, y, c: (x, (y + d) % 4, c))
            else:
                perm = wide_perm(lambda x, y, c: ((x + d) % 4, y, c))
            got.append(lax.ppermute(part, "wide", perm))
        if axis == 0:
            part = (part + got[0]) + (got[1] + got[2])
    return [part] + got


def shards(volume, log_weights, means, prec_factor):
    rows = jnp.transpose(volume, (1, 0, 2))
    head, tail = pack(rows)
    left, right = neighbours(tail, head, "narrow")
    lhs, prior = prepare(log_weights, means, prec_factor)
    left, right, lhs = lax.optimization_barrier((left, right, lhs))
    bottom = jnp.concatenate([rows[ROWS - MARGIN :], left[6:], right[6:]], axis=0)
    top = jnp.concatenate([rows[:MARGIN], left[:2], right[:2]], axis=0)
    before, after = neighbours(bottom, top, "wide")
    responsibility, moments = local_step((before, rows, after, left, right), lhs, prior)
    return (responsibility,) + finish(*device_sum(moments))


def solution(mesh):
    in_specs = (P(None, "wide", "narrow"), P(), P(), P())
    out_specs = (P(None, None, "wide", "narrow"), P(), P(), P())
    return jax.shard_map(shards, mesh=mesh, in_specs=in_specs, out_specs=out_specs, check_vma=False)
```

```python
import math

import jax
import jax.numpy as jnp
import numpy as np
from jax import lax
from jax.experimental import pallas as pl
from jax.experimental.pallas import tpu as pltpu
from jax.sharding import PartitionSpec as P

BASE_TAPS = ((1.0, 4.0, 6.0, 4.0, 1.0), (-1.0, -2.0, 0.0, 2.0, 1.0), (1.0, 0.0, -2.0, 0.0, 1.0))
TAP_NORMS = (70.0, 10.0, 6.0)
DILATIONS = (1, 2, 4, 8)
ORDER_TRIPLES = (
    (0, 0, 0),
    (0, 1, 0),
    (0, 0, 1),
    (1, 0, 0),
    (0, 2, 0),
    (0, 0, 2),
    (2, 0, 0),
    (0, 1, 1),
    (1, 1, 0),
    (1, 0, 1),
    (1, 1, 1),
    (0, 2, 2),
)
SHIFTS = (-16, -8, -4, -2, -1, 0, 1, 2, 4, 8, 16)
MARGIN = 16
PLANES, ROWS, COLS = 16, 64, 128
COMP, FEAT = 6, 48
DEEP = 4 * FEAT + 16


def filter_matrix():
    out = np.zeros((4, 12 * PLANES, 5, 5, PLANES), np.float32)
    for s, d in enumerate(DILATIONS):
        for j, (oz, ox, oy) in enumerate(ORDER_TRIPLES):
            plane_taps = np.outer(BASE_TAPS[ox], BASE_TAPS[oy])
            for c in range(5):
                for z in range(PLANES):
                    if s % 2 == 0:
                        main, slot, other = j, z % 2, j - 8
                    else:
                        main, slot, other = j - 4, 1 - z % 2, j
                    if 0 <= main < 8:
                        row = 8 * z + main
                    else:
                        row = 8 * PLANES + z // 2 * 8 + slot * 4 + other
                    src = z + (c - 2) * d
                    if 0 <= src < PLANES:
                        out[s, row, :, :, src] += BASE_TAPS[oz][c] * plane_taps
    return out.reshape(4, 12 * PLANES, 25 * PLANES)


def kernel(
    before_ref,
    rows_ref,
    after_ref,
    left_ref,
    right_ref,
    filt_in,
    scale_ref,
    lhs_ref,
    prior_ref,
    resp_ref,
    moment_ref,
    shifted,
    feats,
    sec_ref,
    cnt_ref,
    filt_ref,
    semaphore,
):
    octet = pl.program_id(0)
    one_tile = jnp.where(lax.broadcasted_iota(jnp.int32, (16, COLS), 0) < 3, 1.0, 0.0)
    one_tile = one_tile.astype(jnp.bfloat16)

    @pl.when(octet == 0)
    def _():
        taps_copy = pltpu.make_async_copy(filt_in, filt_ref, semaphore)
        taps_copy.start()

        def fill(x, get_row, left, right):
            for m in range(8):
                row = get_row(m)
                for n, shift in enumerate(SHIFTS):
                    if shift < 0:
                        edge = left[:, 16 * m + 16 + shift : 16 * m + 16]
                        moved = jnp.concatenate([edge, row[:, : COLS + shift]], axis=1)
                    elif shift > 0:
                        edge = right[:, 16 * m : 16 * m + shift]
                        moved = jnp.concatenate([row[:, shift:], edge], axis=1)
                    else:
                        moved = row
                    shifted[n, x + m] = moved

        for g in range(2):
            get_before = lambda m: before_ref[8 * g + m]
            get_after = lambda m: after_ref[8 * g + m]
            fill(8 * g, get_before, before_ref[16 + g], before_ref[18 + g])
            fill(MARGIN + ROWS + 8 * g, get_after, after_ref[16 + g], after_ref[18 + g])

        def one_group(g, carry):
            fill(MARGIN + 8 * g, lambda m: rows_ref[8 * g + m], left_ref[g], right_ref[g])
            return carry

        lax.fori_loop(0, ROWS // 8, one_group, 0, unroll=2)
        sec_ref[...] = jnp.zeros_like(sec_ref)
        cnt_ref[...] = jnp.zeros_like(cnt_ref)
        taps_copy.wait()

    def one_pair(pair, carry):
        x = octet * 8 + pair * 2
        blocks = []
        for s, d in enumerate(DILATIONS):
            sides = []
            for e in range(2):
                tiles = [
                    shifted[SHIFTS.index((b - 2) * d), x + e + MARGIN + (a - 2) * d]
                    for a in range(5)
                    for b in range(5)
                ]
                sides.append(jnp.concatenate(tiles, axis=0))
            rhs = jnp.concatenate(sides, axis=1)
            out = jnp.dot(filt_ref[s], rhs, preferred_element_type=jnp.float32)
            blocks.append(out)
        low = lax.broadcasted_iota(jnp.int32, (PLANES // 2, 8, 2 * COLS), 1) < 4
        rows = []
        for first, second in (blocks[:2], blocks[2:]):
            rows.append(first[: 8 * PLANES].reshape(PLANES, 8, 2 * COLS))
            one = first[8 * PLANES :].reshape(PLANES // 2, 8, 2 * COLS)
            two = second[8 * PLANES :].reshape(PLANES // 2, 8, 2 * COLS)
            even = jnp.where(low, one, two)
            odd = jnp.where(low, two, one)
            odd = jnp.concatenate([odd[:, 4:], odd[:, :4]], axis=1)
            rows.append(jnp.stack([even, odd], axis=1).reshape(PLANES, 8, 2 * COLS))
            rows.append(second[: 8 * PLANES].reshape(PLANES, 8, 2 * COLS))
        whole = jnp.concatenate(rows, axis=1)
        for e in range(2):
            part = whole[:, :, e * COLS : (e + 1) * COLS] * scale_ref[...][None]
            feats[pair * 2 + e] = part.astype(jnp.bfloat16)
        return carry

    lax.fori_loop(0, 4, one_pair, 0, unroll=4)

    def expect(z):
        quads = []
        for q in range(2):
            quads.append(
                jnp.concatenate([feats[4 * q + i, z] for i in range(4)] + [one_tile], axis=0)
            )
        rhs = jnp.concatenate(quads, axis=1)
        scores = []
        for g in range(3):
            proj = jnp.dot(
                lhs_ref[g * 8 * FEAT : (g + 1) * 8 * FEAT], rhs, preferred_element_type=jnp.float32
            )
            proj = proj.reshape(FEAT, 8, 2 * COLS)
            distance = jnp.sum(proj * proj, axis=0)
            prior = prior_ref[g]
            scores.append(jnp.concatenate([prior, prior], axis=1) - 0.5 * distance)
        top = jnp.maximum(jnp.maximum(scores[0], scores[1]), scores[2])
        top = jnp.maximum(top, pltpu.roll(top, 4, 0))
        powers = [jnp.exp(s - top) for s in scores]
        total = powers[0] + powers[1] + powers[2]
        total = total + pltpu.roll(total, 4, 0)
        inverse = 1.0 / total
        for g in range(3):
            r = powers[g] * inverse
            left, right = r[:, :COLS], r[:, COLS:]
            for h in range(2):
                tile = jnp.concatenate(
                    [left[4 * h : 4 * h + 4], right[4 * h : 4 * h + 4]], axis=0
                )
                resp_ref[2 * g + h, z] = tile
                cnt_ref[2 * g + h] += tile

    def moment(z):
        features, weighted = [], []
        tiles = [resp_ref[k, z] for k in range(COMP)]
        for i in range(8):
            f = feats[i, z]
            f32 = f.astype(jnp.float32)
            features.append(jnp.concatenate([f, one_tile], axis=0))
            weighted.append(
                jnp.concatenate(
                    [(tiles[k][i : i + 1] * f32).astype(jnp.bfloat16) for k in range(COMP)],
                    axis=0,
                )
            )
        f_all = jnp.concatenate(features, axis=1)
        w_all = jnp.concatenate(weighted, axis=1)
        sec_ref[...] += lax.dot_general(
            w_all, f_all, (((1,), (1,)), ((), ())), preferred_element_type=jnp.float32
        )

    def expect_step(z, carry):
        expect(z)
        return carry

    def moment_step(z, carry):
        moment(z)
        return carry

    lax.fori_loop(0, PLANES, expect_step, 0, unroll=16)
    lax.fori_loop(0, PLANES, moment_step, 0, unroll=16)

    @pl.when(octet == pl.num_programs(0) - 1)
    def _():
        lane = lax.broadcasted_iota(jnp.int32, (FEAT, 128), 1)
        for m in range(3):
            first, second = [sec_ref[k * FEAT : (k + 1) * FEAT] for k in (2 * m, 2 * m + 1)]
            both = jnp.concatenate([first, second], axis=1)
            both = jnp.where(lane == FEAT + 1, jnp.sum(cnt_ref[2 * m]), both)
            both = jnp.where(lane == 64 + FEAT + 1, jnp.sum(cnt_ref[2 * m + 1]), both)
            moment_ref[m * FEAT : (m + 1) * FEAT] = both


def prepare_kernel(weight_ref, mean_ref, factor_ref, lhs_ref, prior_ref, scale_ref):
    logits = weight_ref[...]
    top = jnp.max(logits, axis=1, keepdims=True)
    log_total = jnp.log(jnp.sum(jnp.exp(logits - top), axis=1, keepdims=True)) + top
    on_diagonal = lax.broadcasted_iota(jnp.int32, (FEAT, FEAT), 0) == lax.broadcasted_iota(
        jnp.int32, (FEAT, FEAT), 1
    )
    lane = lax.broadcasted_iota(jnp.int32, (FEAT, 256), 1)
    half = lax.broadcasted_iota(jnp.int32, (8, COLS), 0) < 4
    to_row = lax.broadcasted_iota(jnp.int32, (8 * FEAT, 8 * FEAT), 0)
    from_row = lax.broadcasted_iota(jnp.int32, (8 * FEAT, 8 * FEAT), 1)
    wanted = (to_row & 7) * FEAT + (to_row >> 3)
    order = jnp.where(wanted == from_row, 1.0, 0.0).astype(jnp.bfloat16)
    feature = lax.broadcasted_iota(jnp.int32, (FEAT, COLS), 0)
    for j, (oz, ox, oy) in enumerate(ORDER_TRIPLES):
        value = 1.0 / math.sqrt(TAP_NORMS[oz] * TAP_NORMS[ox] * TAP_NORMS[oy])
        scale = jnp.full((FEAT, COLS), value, jnp.float32) if j == 0 else jnp.where(lax.rem(feature, len(ORDER_TRIPLES)) == j, value, scale)
    scale_ref[...] = scale
    for g in range(3):
        rows, priors = [], []
        for h in range(2):
            k = 2 * g + h
            factor = factor_ref[k]
            log_diag = jnp.sum(jnp.where(on_diagonal, jnp.log(jnp.where(on_diagonal, factor, 1.0)), 0.0))
            prior = logits[:, k : k + 1] - log_total + log_diag - 0.5 * FEAT * math.log(2.0 * math.pi)
            priors.append(jnp.broadcast_to(prior, (8, COLS)))
            columns = factor.astype(jnp.bfloat16).astype(jnp.float32).T
            offset = jnp.sum(columns * mean_ref[k : k + 1], axis=1, keepdims=True)
            rest = -offset
            tail = jnp.zeros((FEAT, 256), jnp.float32)
            for t in range(3):
                term = rest.astype(jnp.bfloat16).astype(jnp.float32)
                tail = jnp.where(lane == 4 * FEAT + t, term, tail)
                rest = rest - term
            wide = jnp.concatenate([columns, jnp.zeros((FEAT, 256 - FEAT), jnp.float32)], axis=1)
            for x in range(4):
                moved = wide if x == 0 else pltpu.roll(wide, x * FEAT, 1)
                rows.append((moved + tail).astype(jnp.bfloat16))
        block = jnp.dot(order, jnp.concatenate(rows, axis=0), preferred_element_type=jnp.float32)
        lhs_ref[g * 8 * FEAT : (g + 1) * 8 * FEAT] = block[:, :DEEP].astype(jnp.bfloat16)
        prior_ref[g] = jnp.where(half, priors[0], priors[1])


def vmem_specs(count):
    return [pl.BlockSpec(memory_space=pltpu.VMEM)] * count


def prepare(log_weights, means, prec_factor):
    return pl.pallas_call(
        prepare_kernel,
        in_specs=vmem_specs(3),
        out_specs=vmem_specs(3),
        out_shape=[
            jax.ShapeDtypeStruct((COMP * FEAT * 4, DEEP), jnp.bfloat16),
            jax.ShapeDtypeStruct((3, 8, COLS), jnp.float32),
            jax.ShapeDtypeStruct((FEAT, COLS), jnp.float32),
        ],
        cost_estimate=pl.CostEstimate(flops=10**8, bytes_accessed=2 * 10**6, transcendentals=2 * 10**4),
        compiler_params=pltpu.CompilerParams(vmem_limit_bytes=8 * 2**20),
        name="prepare",
    )(log_weights.reshape(1, COMP), means, prec_factor)


def finish_kernel(a_ref, b_ref, c_ref, d_ref, weight_ref, mean_ref, cov_ref):
    on_diagonal = lax.broadcasted_iota(jnp.int32, (FEAT, FEAT), 0) == lax.broadcasted_iota(
        jnp.int32, (FEAT, FEAT), 1
    )
    lane = lax.broadcasted_iota(jnp.int32, (1, COMP), 1)
    counts = jnp.zeros((1, COMP), jnp.float32)
    for k in range(COMP):
        at = slice(k // 2 * FEAT, (k // 2 + 1) * FEAT)
        both = (a_ref[at] + b_ref[at]) + (c_ref[at] + d_ref[at])
        block = both[:, k % 2 * 64 : k % 2 * 64 + 64]
        count = block[:1, FEAT + 1 : FEAT + 2]
        column = block[:, FEAT : FEAT + 1] / count
        row = jnp.sum(jnp.where(on_diagonal, column, 0.0), axis=0, keepdims=True)
        cov_ref[k] = block[:, :FEAT] / count - column * row
        mean_ref[k : k + 1] = row
        counts = jnp.where(lane == k, count, counts)
    weight_ref[...] = counts / jnp.sum(counts, axis=1, keepdims=True)


def finish(*parts):
    new_weights, new_means, new_cov = pl.pallas_call(
        finish_kernel,
        in_specs=vmem_specs(4),
        out_specs=vmem_specs(3),
        out_shape=[
            jax.ShapeDtypeStruct((1, COMP), jnp.float32),
            jax.ShapeDtypeStruct((COMP, FEAT), jnp.float32),
            jax.ShapeDtypeStruct((COMP, FEAT, FEAT), jnp.float32),
        ],
        compiler_params=pltpu.CompilerParams(vmem_limit_bytes=8 * 2**20),
        name="finish",
    )(*parts)
    return new_weights.reshape(COMP), new_means, new_cov


def local_step(pieces, lhs, prior, scale):
    filt = jnp.asarray(filter_matrix(), jnp.bfloat16)
    full = lambda *shape: pl.BlockSpec(shape, lambda o: (0,) * len(shape))
    return pl.pallas_call(
        kernel,
        grid=(ROWS // 8,),
        in_specs=[
            *[full(*piece.shape) for piece in pieces],
            pl.BlockSpec(memory_space=pltpu.HBM),
            full(*scale.shape),
            full(*lhs.shape),
            full(*prior.shape),
        ],
        out_specs=[
            pl.BlockSpec((COMP, PLANES, 8, COLS), lambda o: (0, 0, o, 0)),
            full(3 * FEAT, 128),
        ],
        out_shape=[
            jax.ShapeDtypeStruct((COMP, PLANES, ROWS, COLS), jnp.float32),
            jax.ShapeDtypeStruct((3 * FEAT, 128), jnp.float32),
        ],
        scratch_shapes=[
            pltpu.VMEM((len(SHIFTS), ROWS + 2 * MARGIN, PLANES, COLS), jnp.bfloat16),
            pltpu.VMEM((8, PLANES, FEAT, COLS), jnp.bfloat16),
            pltpu.VMEM((COMP * FEAT, FEAT + 16), jnp.float32),
            pltpu.VMEM((COMP, 8, COLS), jnp.float32),
            pltpu.VMEM(filt.shape, filt.dtype),
            pltpu.SemaphoreType.DMA,
        ],
        compiler_params=pltpu.CompilerParams(
            dimension_semantics=("arbitrary",), vmem_limit_bytes=32 * 2**20
        ),
        name="mixture_step",
    )(*pieces, filt, scale, lhs, prior)


def pack_kernel(rows_ref, head_ref, tail_ref):
    for n in range(ROWS // 8):
        group = [rows_ref[8 * n + m] for m in range(8)]
        head_ref[n] = jnp.concatenate([row[:, :MARGIN] for row in group], axis=1)
        tail_ref[n] = jnp.concatenate([row[:, COLS - MARGIN :] for row in group], axis=1)


def pack(rows):
    shape = jax.ShapeDtypeStruct((ROWS // 8, PLANES, COLS), jnp.bfloat16)
    return pl.pallas_call(
        pack_kernel,
        in_specs=vmem_specs(1),
        out_specs=vmem_specs(2),
        out_shape=[shape, shape],
        compiler_params=pltpu.CompilerParams(vmem_limit_bytes=8 * 2**20),
        name="pack",
    )(rows)


def neighbours(to_next, to_previous, axis):
    ends = lax.axis_size(axis) - 1
    before = lax.ppermute(to_next, axis, [(i, i + 1) for i in range(ends)])
    after = lax.ppermute(to_previous, axis, [(i + 1, i) for i in range(ends)])
    return before, after


def wide_perm(move):
    perm = []
    for i in range(32):
        x, y, c = move(i // 8, (i // 2) % 4, i % 2)
        perm.append((i, (x * 4 + y) * 2 + c))
    return perm


def device_sum(part):
    part = part + lax.ppermute(part, "wide", wide_perm(lambda x, y, c: (x, y, 1 - c)))
    narrow = [
        lax.ppermute(part, "narrow", [(i, (i + d) % 4) for i in range(4)]) for d in (1, 2, 3)
    ]
    part = ((part + narrow[0]) + (narrow[1] + narrow[2]))
    for axis in range(2):
        got = []
        for d in (1, 2, 3):
            if axis == 0:
                perm = wide_perm(lambda x, y, c: (x, (y + d) % 4, c))
            else:
                perm = wide_perm(lambda x, y, c: ((x + d) % 4, y, c))
            got.append(lax.ppermute(part, "wide", perm))
        if axis == 0:
            part = (part + got[0]) + (got[1] + got[2])
    return [part] + got


def shards(volume, log_weights, means, prec_factor):
    rows = jnp.transpose(volume, (1, 0, 2))
    head, tail = pack(rows)
    left, right = neighbours(tail, head, "narrow")
    lhs, prior, scale = prepare(log_weights, means, prec_factor)
    bottom = jnp.concatenate([rows[ROWS - MARGIN :], left[6:], right[6:]], axis=0)
    top = jnp.concatenate([rows[:MARGIN], left[:2], right[:2]], axis=0)
    before, after = neighbours(bottom, top, "wide")
    responsibility, moments = local_step((before, rows, after, left, right), lhs, prior, scale)
    return (responsibility,) + finish(*device_sum(moments))


def solution(mesh):
    in_specs = (P(None, "wide", "narrow"), P(), P(), P())
    out_specs = (P(None, None, "wide", "narrow"), P(), P(), P())
    return jax.shard_map(shards, mesh=mesh, in_specs=in_specs, out_specs=out_specs, check_vma=False)
```

```python
import math

import jax
import jax.numpy as jnp
import numpy as np
from jax import lax
from jax.experimental import pallas as pl
from jax.experimental.pallas import tpu as pltpu
from jax.sharding import PartitionSpec as P

BASE_TAPS = ((1.0, 4.0, 6.0, 4.0, 1.0), (-1.0, -2.0, 0.0, 2.0, 1.0), (1.0, 0.0, -2.0, 0.0, 1.0))
TAP_NORMS = (70.0, 10.0, 6.0)
DILATIONS = (1, 2, 4, 8)
ORDER_TRIPLES = (
    (0, 0, 0),
    (0, 1, 0),
    (0, 0, 1),
    (1, 0, 0),
    (0, 2, 0),
    (0, 0, 2),
    (2, 0, 0),
    (0, 1, 1),
    (1, 1, 0),
    (1, 0, 1),
    (1, 1, 1),
    (0, 2, 2),
)
SHIFTS = (-16, -8, -4, -2, -1, 0, 1, 2, 4, 8, 16)
MARGIN = 16
PLANES, ROWS, COLS = 16, 64, 128
COMP, FEAT = 6, 48
DEEP = 4 * FEAT + 16


def filter_matrix():
    out = np.zeros((4, 12 * PLANES, 5, 5, PLANES), np.float32)
    for s, d in enumerate(DILATIONS):
        for j, (oz, ox, oy) in enumerate(ORDER_TRIPLES):
            plane_taps = np.outer(BASE_TAPS[ox], BASE_TAPS[oy])
            for c in range(5):
                for z in range(PLANES):
                    if s % 2 == 0:
                        main, slot, other = j, z % 2, j - 8
                    else:
                        main, slot, other = j - 4, 1 - z % 2, j
                    if 0 <= main < 8:
                        row = 8 * z + main
                    else:
                        row = 8 * PLANES + z // 2 * 8 + slot * 4 + other
                    src = z + (c - 2) * d
                    if 0 <= src < PLANES:
                        out[s, row, :, :, src] += BASE_TAPS[oz][c] * plane_taps
    return out.reshape(4, 12 * PLANES, 25 * PLANES)


def kernel(
    before_ref,
    rows_ref,
    after_ref,
    left_ref,
    right_ref,
    filt_in,
    scale_ref,
    lhs_ref,
    prior_ref,
    resp_ref,
    moment_ref,
    shifted,
    feats,
    sec_ref,
    cnt_ref,
    filt_ref,
    semaphore,
):
    octet = pl.program_id(0)
    one_tile = jnp.where(lax.broadcasted_iota(jnp.int32, (16, COLS), 0) < 3, 1.0, 0.0)
    one_tile = one_tile.astype(jnp.bfloat16)

    @pl.when(octet == 0)
    def _():
        taps_copy = pltpu.make_async_copy(filt_in, filt_ref, semaphore)
        taps_copy.start()

        def fill(x, get_row, left, right):
            for m in range(8):
                row = get_row(m)
                for n, shift in enumerate(SHIFTS):
                    if shift < 0:
                        edge = left[:, 16 * m + 16 + shift : 16 * m + 16]
                        moved = jnp.concatenate([edge, row[:, : COLS + shift]], axis=1)
                    elif shift > 0:
                        edge = right[:, 16 * m : 16 * m + shift]
                        moved = jnp.concatenate([row[:, shift:], edge], axis=1)
                    else:
                        moved = row
                    shifted[n, x + m] = moved

        for g in range(2):
            get_before = lambda m: before_ref[8 * g + m]
            get_after = lambda m: after_ref[8 * g + m]
            fill(8 * g, get_before, before_ref[16 + g], before_ref[18 + g])
            fill(MARGIN + ROWS + 8 * g, get_after, after_ref[16 + g], after_ref[18 + g])

        def one_group(g, carry):
            fill(MARGIN + 8 * g, lambda m: rows_ref[8 * g + m], left_ref[g], right_ref[g])
            return carry

        lax.fori_loop(0, ROWS // 8, one_group, 0, unroll=2)
        sec_ref[...] = jnp.zeros_like(sec_ref)
        cnt_ref[...] = jnp.zeros_like(cnt_ref)
        taps_copy.wait()

    def one_pair(pair, carry):
        x = octet * 8 + pair * 2
        blocks = []
        for s, d in enumerate(DILATIONS):
            sides = []
            for e in range(2):
                tiles = [
                    shifted[SHIFTS.index((b - 2) * d), x + e + MARGIN + (a - 2) * d]
                    for a in range(5)
                    for b in range(5)
                ]
                sides.append(jnp.concatenate(tiles, axis=0))
            rhs = jnp.concatenate(sides, axis=1)
            out = jnp.dot(filt_ref[s], rhs, preferred_element_type=jnp.float32)
            blocks.append(out)
        low = lax.broadcasted_iota(jnp.int32, (PLANES // 2, 8, 2 * COLS), 1) < 4
        rows = []
        for first, second in (blocks[:2], blocks[2:]):
            rows.append(first[: 8 * PLANES].reshape(PLANES, 8, 2 * COLS))
            one = first[8 * PLANES :].reshape(PLANES // 2, 8, 2 * COLS)
            two = second[8 * PLANES :].reshape(PLANES // 2, 8, 2 * COLS)
            even = jnp.where(low, one, two)
            odd = jnp.where(low, two, one)
            odd = jnp.concatenate([odd[:, 4:], odd[:, :4]], axis=1)
            rows.append(jnp.stack([even, odd], axis=1).reshape(PLANES, 8, 2 * COLS))
            rows.append(second[: 8 * PLANES].reshape(PLANES, 8, 2 * COLS))
        whole = jnp.concatenate(rows, axis=1)
        for e in range(2):
            part = whole[:, :, e * COLS : (e + 1) * COLS] * scale_ref[...][None]
            feats[pair * 2 + e] = part.astype(jnp.bfloat16)
        return carry

    lax.fori_loop(0, 4, one_pair, 0, unroll=4)

    def expect(z):
        quads = []
        for q in range(2):
            quads.append(
                jnp.concatenate([feats[4 * q + i, z] for i in range(4)] + [one_tile], axis=0)
            )
        rhs = jnp.concatenate(quads, axis=1)
        scores = []
        for g in range(3):
            proj = jnp.dot(
                lhs_ref[g * 8 * FEAT : (g + 1) * 8 * FEAT], rhs, preferred_element_type=jnp.float32
            )
            proj = proj.reshape(FEAT, 8, 2 * COLS)
            distance = jnp.sum(proj * proj, axis=0)
            prior = prior_ref[g]
            scores.append(jnp.concatenate([prior, prior], axis=1) - 0.5 * distance)
        top = jnp.maximum(jnp.maximum(scores[0], scores[1]), scores[2])
        top = jnp.maximum(top, pltpu.roll(top, 4, 0))
        powers = [jnp.exp(s - top) for s in scores]
        total = powers[0] + powers[1] + powers[2]
        total = total + pltpu.roll(total, 4, 0)
        inverse = 1.0 / total
        for g in range(3):
            r = powers[g] * inverse
            left, right = r[:, :COLS], r[:, COLS:]
            for h in range(2):
                tile = jnp.concatenate(
                    [left[4 * h : 4 * h + 4], right[4 * h : 4 * h + 4]], axis=0
                )
                resp_ref[2 * g + h, z] = tile
                cnt_ref[2 * g + h] += tile

    def moment(z):
        features, weighted = [], []
        tiles = [resp_ref[k, z] for k in range(COMP)]
        for i in range(8):
            f = feats[i, z]
            f32 = f.astype(jnp.float32)
            features.append(jnp.concatenate([f, one_tile], axis=0))
            weighted.append(
                jnp.concatenate(
                    [(tiles[k][i : i + 1] * f32).astype(jnp.bfloat16) for k in range(COMP)],
                    axis=0,
                )
            )
        f_all = jnp.concatenate(features, axis=1)
        w_all = jnp.concatenate(weighted, axis=1)
        sec_ref[...] += lax.dot_general(
            w_all, f_all, (((1,), (1,)), ((), ())), preferred_element_type=jnp.float32
        )

    def expect_step(z, carry):
        expect(z)
        return carry

    def moment_step(z, carry):
        moment(z)
        return carry

    lax.fori_loop(0, PLANES, expect_step, 0, unroll=16)
    lax.fori_loop(0, PLANES, moment_step, 0, unroll=16)

    @pl.when(octet == pl.num_programs(0) - 1)
    def _():
        half = FEAT // 2
        row = lax.broadcasted_iota(jnp.int32, (half, 64), 0)
        lane = lax.broadcasted_iota(jnp.int32, (half, 64), 1)
        packed = []
        for k in range(COMP):
            upper = sec_ref[k * FEAT : k * FEAT + half]
            lower = sec_ref[k * FEAT + half : (k + 1) * FEAT]
            first = lower[:, FEAT : FEAT + 1]
            diagonal = jnp.sum(jnp.where(lane == row + half, lower, 0.0), axis=1, keepdims=True)
            block = jnp.where(lane < row, jnp.concatenate([lower[:, half:], lower[:, :half]], axis=1), upper)
            block = jnp.where(lane == FEAT + 1, first, block)
            block = jnp.where(lane == FEAT + 2, diagonal, block)
            packed.append(jnp.where(lane == FEAT + 3, jnp.sum(cnt_ref[k]), block))
        for m in range(3):
            both = jnp.concatenate(packed[2 * m : 2 * m + 2], axis=1)
            moment_ref[m * half : (m + 1) * half] = both


def prepare_kernel(weight_ref, mean_ref, factor_ref, lhs_ref, prior_ref, scale_ref):
    logits = weight_ref[...]
    top = jnp.max(logits, axis=1, keepdims=True)
    log_total = jnp.log(jnp.sum(jnp.exp(logits - top), axis=1, keepdims=True)) + top
    on_diagonal = lax.broadcasted_iota(jnp.int32, (FEAT, FEAT), 0) == lax.broadcasted_iota(
        jnp.int32, (FEAT, FEAT), 1
    )
    lane = lax.broadcasted_iota(jnp.int32, (FEAT, 256), 1)
    half = lax.broadcasted_iota(jnp.int32, (8, COLS), 0) < 4
    to_row = lax.broadcasted_iota(jnp.int32, (8 * FEAT, 8 * FEAT), 0)
    from_row = lax.broadcasted_iota(jnp.int32, (8 * FEAT, 8 * FEAT), 1)
    wanted = (to_row & 7) * FEAT + (to_row >> 3)
    order = jnp.where(wanted == from_row, 1.0, 0.0).astype(jnp.bfloat16)
    feature = lax.broadcasted_iota(jnp.int32, (FEAT, COLS), 0)
    for j, (oz, ox, oy) in enumerate(ORDER_TRIPLES):
        value = 1.0 / math.sqrt(TAP_NORMS[oz] * TAP_NORMS[ox] * TAP_NORMS[oy])
        scale = jnp.full((FEAT, COLS), value, jnp.float32) if j == 0 else jnp.where(lax.rem(feature, len(ORDER_TRIPLES)) == j, value, scale)
    scale_ref[...] = scale
    for g in range(3):
        rows, priors = [], []
        for h in range(2):
            k = 2 * g + h
            factor = factor_ref[k]
            log_diag = jnp.sum(jnp.where(on_diagonal, jnp.log(jnp.where(on_diagonal, factor, 1.0)), 0.0))
            prior = logits[:, k : k + 1] - log_total + log_diag - 0.5 * FEAT * math.log(2.0 * math.pi)
            priors.append(jnp.broadcast_to(prior, (8, COLS)))
            columns = factor.astype(jnp.bfloat16).astype(jnp.float32).T
            offset = jnp.sum(columns * mean_ref[k : k + 1], axis=1, keepdims=True)
            rest = -offset
            tail = jnp.zeros((FEAT, 256), jnp.float32)
            for t in range(3):
                term = rest.astype(jnp.bfloat16).astype(jnp.float32)
                tail = jnp.where(lane == 4 * FEAT + t, term, tail)
                rest = rest - term
            wide = jnp.concatenate([columns, jnp.zeros((FEAT, 256 - FEAT), jnp.float32)], axis=1)
            for x in range(4):
                moved = wide if x == 0 else pltpu.roll(wide, x * FEAT, 1)
                rows.append((moved + tail).astype(jnp.bfloat16))
        block = jnp.dot(order, jnp.concatenate(rows, axis=0), preferred_element_type=jnp.float32)
        lhs_ref[g * 8 * FEAT : (g + 1) * 8 * FEAT] = block[:, :DEEP].astype(jnp.bfloat16)
        prior_ref[g] = jnp.where(half, priors[0], priors[1])


def vmem_specs(count):
    return [pl.BlockSpec(memory_space=pltpu.VMEM)] * count


def prepare(log_weights, means, prec_factor):
    return pl.pallas_call(
        prepare_kernel,
        in_specs=vmem_specs(3),
        out_specs=vmem_specs(3),
        out_shape=[
            jax.ShapeDtypeStruct((COMP * FEAT * 4, DEEP), jnp.bfloat16),
            jax.ShapeDtypeStruct((3, 8, COLS), jnp.float32),
            jax.ShapeDtypeStruct((FEAT, COLS), jnp.float32),
        ],
        cost_estimate=pl.CostEstimate(flops=10**8, bytes_accessed=2 * 10**6, transcendentals=2 * 10**4),
        compiler_params=pltpu.CompilerParams(vmem_limit_bytes=8 * 2**20),
        name="prepare",
    )(log_weights.reshape(1, COMP), means, prec_factor)


def pick(block, column):
    lane = lax.broadcasted_iota(jnp.int32, block.shape, 1)
    return jnp.sum(jnp.where(lane == column, block, 0.0), axis=1, keepdims=True)


def finish_kernel(a_ref, b_ref, c_ref, d_ref, weight_ref, mean_ref, cov_ref):
    half = FEAT // 2
    row = lax.broadcasted_iota(jnp.int32, (FEAT, FEAT), 0)
    col = lax.broadcasted_iota(jnp.int32, (FEAT, FEAT), 1)
    stored = ((row < half) & (col >= row)) | ((row >= half) & (col >= half) & (col < row))
    lane = lax.broadcasted_iota(jnp.int32, (1, COMP), 1)
    counts = jnp.zeros((1, COMP), jnp.float32)
    for k in range(COMP):
        at = slice(k // 2 * half, (k // 2 + 1) * half)
        both = (a_ref[at] + b_ref[at]) + (c_ref[at] + d_ref[at])
        block = both if k % 2 == 0 else pltpu.roll(both, 64, 1)
        upper = block[:, :FEAT]
        lower = pltpu.roll(block, half, 1)[:, :FEAT]
        second = jnp.concatenate([upper, lower], axis=0)
        second = jnp.where(stored, second, second.T)
        diagonal = pick(block, FEAT + 2)
        diagonal = jnp.concatenate([diagonal, diagonal], axis=0)
        second = jnp.where((row == col) & (row >= half), diagonal, second)
        first = jnp.concatenate([pick(block, FEAT), pick(block, FEAT + 1)], axis=0)
        count = pick(block, FEAT + 3)[:1]
        column = first / count
        across = jnp.sum(jnp.where(row == col, column, 0.0), axis=0, keepdims=True)
        cov_ref[k] = second / count - column * across
        mean_ref[k : k + 1] = across
        counts = jnp.where(lane == k, count, counts)
    weight_ref[...] = counts / jnp.sum(counts, axis=1, keepdims=True)


def finish(*parts):
    new_weights, new_means, new_cov = pl.pallas_call(
        finish_kernel,
        in_specs=vmem_specs(4),
        out_specs=vmem_specs(3),
        out_shape=[
            jax.ShapeDtypeStruct((1, COMP), jnp.float32),
            jax.ShapeDtypeStruct((COMP, FEAT), jnp.float32),
            jax.ShapeDtypeStruct((COMP, FEAT, FEAT), jnp.float32),
        ],
        compiler_params=pltpu.CompilerParams(vmem_limit_bytes=8 * 2**20),
        name="finish",
    )(*parts)
    return new_weights.reshape(COMP), new_means, new_cov


def local_step(pieces, lhs, prior, scale):
    filt = jnp.asarray(filter_matrix(), jnp.bfloat16)
    full = lambda *shape: pl.BlockSpec(shape, lambda o: (0,) * len(shape))
    return pl.pallas_call(
        kernel,
        grid=(ROWS // 8,),
        in_specs=[
            *[full(*piece.shape) for piece in pieces],
            pl.BlockSpec(memory_space=pltpu.HBM),
            full(*scale.shape),
            full(*lhs.shape),
            full(*prior.shape),
        ],
        out_specs=[
            pl.BlockSpec((COMP, PLANES, 8, COLS), lambda o: (0, 0, o, 0)),
            full(3 * FEAT // 2, 128),
        ],
        out_shape=[
            jax.ShapeDtypeStruct((COMP, PLANES, ROWS, COLS), jnp.float32),
            jax.ShapeDtypeStruct((3 * FEAT // 2, 128), jnp.float32),
        ],
        scratch_shapes=[
            pltpu.VMEM((len(SHIFTS), ROWS + 2 * MARGIN, PLANES, COLS), jnp.bfloat16),
            pltpu.VMEM((8, PLANES, FEAT, COLS), jnp.bfloat16),
            pltpu.VMEM((COMP * FEAT, FEAT + 16), jnp.float32),
            pltpu.VMEM((COMP, 8, COLS), jnp.float32),
            pltpu.VMEM(filt.shape, filt.dtype),
            pltpu.SemaphoreType.DMA,
        ],
        compiler_params=pltpu.CompilerParams(
            dimension_semantics=("arbitrary",), vmem_limit_bytes=32 * 2**20
        ),
        name="mixture_step",
    )(*pieces, filt, scale, lhs, prior)


def pack_kernel(rows_ref, head_ref, tail_ref):
    for n in range(ROWS // 8):
        group = [rows_ref[8 * n + m] for m in range(8)]
        head_ref[n] = jnp.concatenate([row[:, :MARGIN] for row in group], axis=1)
        tail_ref[n] = jnp.concatenate([row[:, COLS - MARGIN :] for row in group], axis=1)


def pack(rows):
    shape = jax.ShapeDtypeStruct((ROWS // 8, PLANES, COLS), jnp.bfloat16)
    return pl.pallas_call(
        pack_kernel,
        in_specs=vmem_specs(1),
        out_specs=vmem_specs(2),
        out_shape=[shape, shape],
        compiler_params=pltpu.CompilerParams(vmem_limit_bytes=8 * 2**20),
        name="pack",
    )(rows)


def neighbours(to_next, to_previous, axis):
    ends = lax.axis_size(axis) - 1
    before = lax.ppermute(to_next, axis, [(i, i + 1) for i in range(ends)])
    after = lax.ppermute(to_previous, axis, [(i + 1, i) for i in range(ends)])
    return before, after


def wide_perm(move):
    perm = []
    for i in range(32):
        x, y, c = move(i // 8, (i // 2) % 4, i % 2)
        perm.append((i, (x * 4 + y) * 2 + c))
    return perm


def device_sum(part):
    part = part + lax.ppermute(part, "wide", wide_perm(lambda x, y, c: (x, y, 1 - c)))
    narrow = [
        lax.ppermute(part, "narrow", [(i, (i + d) % 4) for i in range(4)]) for d in (1, 2, 3)
    ]
    part = ((part + narrow[0]) + (narrow[1] + narrow[2]))
    for axis in range(2):
        got = []
        for d in (1, 2, 3):
            if axis == 0:
                perm = wide_perm(lambda x, y, c: (x, (y + d) % 4, c))
            else:
                perm = wide_perm(lambda x, y, c: ((x + d) % 4, y, c))
            got.append(lax.ppermute(part, "wide", perm))
        if axis == 0:
            part = (part + got[0]) + (got[1] + got[2])
    return [part] + got


def shards(volume, log_weights, means, prec_factor):
    rows = jnp.transpose(volume, (1, 0, 2))
    head, tail = pack(rows)
    left, right = neighbours(tail, head, "narrow")
    lhs, prior, scale = prepare(log_weights, means, prec_factor)
    bottom = jnp.concatenate([rows[ROWS - MARGIN :], left[6:], right[6:]], axis=0)
    top = jnp.concatenate([rows[:MARGIN], left[:2], right[:2]], axis=0)
    before, after = neighbours(bottom, top, "wide")
    responsibility, moments = local_step((before, rows, after, left, right), lhs, prior, scale)
    return (responsibility,) + finish(*device_sum(moments))


def solution(mesh):
    in_specs = (P(None, "wide", "narrow"), P(), P(), P())
    out_specs = (P(None, None, "wide", "narrow"), P(), P(), P())
    return jax.shard_map(shards, mesh=mesh, in_specs=in_specs, out_specs=out_specs, check_vma=False)
```

```python
import math

import jax
import jax.numpy as jnp
import numpy as np
from jax import lax
from jax.experimental import pallas as pl
from jax.experimental.pallas import tpu as pltpu
from jax.sharding import PartitionSpec as P

BASE_TAPS = ((1.0, 4.0, 6.0, 4.0, 1.0), (-1.0, -2.0, 0.0, 2.0, 1.0), (1.0, 0.0, -2.0, 0.0, 1.0))
TAP_NORMS = (70.0, 10.0, 6.0)
DILATIONS = (1, 2, 4, 8)
ORDER_TRIPLES = (
    (0, 0, 0),
    (0, 1, 0),
    (0, 0, 1),
    (1, 0, 0),
    (0, 2, 0),
    (0, 0, 2),
    (2, 0, 0),
    (0, 1, 1),
    (1, 1, 0),
    (1, 0, 1),
    (1, 1, 1),
    (0, 2, 2),
)
SHIFTS = (-16, -8, -4, -2, -1, 0, 1, 2, 4, 8, 16)
MARGIN = 16
PLANES, ROWS, COLS = 16, 64, 128
COMP, FEAT = 6, 48
DEEP = 4 * FEAT + 16


def filter_matrix():
    out = np.zeros((4, 12 * PLANES, 5, 5, PLANES), np.float32)
    for s, d in enumerate(DILATIONS):
        for j, (oz, ox, oy) in enumerate(ORDER_TRIPLES):
            plane_taps = np.outer(BASE_TAPS[ox], BASE_TAPS[oy])
            for c in range(5):
                for z in range(PLANES):
                    if s % 2 == 0:
                        main, slot, other = j, z % 2, j - 8
                    else:
                        main, slot, other = j - 4, 1 - z % 2, j
                    if 0 <= main < 8:
                        row = 8 * z + main
                    else:
                        row = 8 * PLANES + z // 2 * 8 + slot * 4 + other
                    src = z + (c - 2) * d
                    if 0 <= src < PLANES:
                        out[s, row, :, :, src] += BASE_TAPS[oz][c] * plane_taps
    return out.reshape(4, 12 * PLANES, 25 * PLANES)


def kernel(
    before_ref,
    rows_ref,
    after_ref,
    left_ref,
    right_ref,
    filt_in,
    scale_ref,
    lhs_ref,
    prior_ref,
    resp_ref,
    moment_ref,
    shifted,
    feats,
    sec_ref,
    cnt_ref,
    filt_ref,
    semaphore,
):
    octet = pl.program_id(0)
    one_tile = jnp.where(lax.broadcasted_iota(jnp.int32, (16, COLS), 0) < 3, 1.0, 0.0)
    one_tile = one_tile.astype(jnp.bfloat16)

    @pl.when(octet == 0)
    def _():
        taps_copy = pltpu.make_async_copy(filt_in, filt_ref, semaphore)
        taps_copy.start()

        def fill(x, get_row, left, right):
            for m in range(8):
                row = get_row(m)
                for n, shift in enumerate(SHIFTS):
                    if shift < 0:
                        edge = left[:, 16 * m + 16 + shift : 16 * m + 16]
                        moved = jnp.concatenate([edge, row[:, : COLS + shift]], axis=1)
                    elif shift > 0:
                        edge = right[:, 16 * m : 16 * m + shift]
                        moved = jnp.concatenate([row[:, shift:], edge], axis=1)
                    else:
                        moved = row
                    shifted[n, x + m] = moved

        for g in range(2):
            get_before = lambda m: before_ref[8 * g + m]
            get_after = lambda m: after_ref[8 * g + m]
            fill(8 * g, get_before, before_ref[16 + g], before_ref[18 + g])
            fill(MARGIN + ROWS + 8 * g, get_after, after_ref[16 + g], after_ref[18 + g])

        def one_group(g, carry):
            fill(MARGIN + 8 * g, lambda m: rows_ref[8 * g + m], left_ref[g], right_ref[g])
            return carry

        lax.fori_loop(0, ROWS // 8, one_group, 0, unroll=2)
        sec_ref[...] = jnp.zeros_like(sec_ref)
        cnt_ref[...] = jnp.zeros_like(cnt_ref)
        taps_copy.wait()

    def one_pair(pair, carry):
        x = octet * 8 + pair * 2
        blocks = []
        for s, d in enumerate(DILATIONS):
            sides = []
            for e in range(2):
                tiles = [
                    shifted[SHIFTS.index((b - 2) * d), x + e + MARGIN + (a - 2) * d]
                    for a in range(5)
                    for b in range(5)
                ]
                sides.append(jnp.concatenate(tiles, axis=0))
            rhs = jnp.concatenate(sides, axis=1)
            out = jnp.dot(filt_ref[s], rhs, preferred_element_type=jnp.float32)
            blocks.append(out)
        low = lax.broadcasted_iota(jnp.int32, (PLANES // 2, 8, 2 * COLS), 1) < 4
        rows = []
        for first, second in (blocks[:2], blocks[2:]):
            rows.append(first[: 8 * PLANES].reshape(PLANES, 8, 2 * COLS))
            one = first[8 * PLANES :].reshape(PLANES // 2, 8, 2 * COLS)
            two = second[8 * PLANES :].reshape(PLANES // 2, 8, 2 * COLS)
            even = jnp.where(low, one, two)
            odd = jnp.where(low, two, one)
            odd = jnp.concatenate([odd[:, 4:], odd[:, :4]], axis=1)
            rows.append(jnp.stack([even, odd], axis=1).reshape(PLANES, 8, 2 * COLS))
            rows.append(second[: 8 * PLANES].reshape(PLANES, 8, 2 * COLS))
        whole = jnp.concatenate(rows, axis=1)
        for e in range(2):
            part = whole[:, :, e * COLS : (e + 1) * COLS] * scale_ref[...][None]
            feats[pair * 2 + e] = part.astype(jnp.bfloat16)
        return carry

    lax.fori_loop(0, 4, one_pair, 0, unroll=4)

    def expect(z):
        quads = []
        for q in range(2):
            quads.append(
                jnp.concatenate([feats[4 * q + i, z] for i in range(4)] + [one_tile], axis=0)
            )
        rhs = jnp.concatenate(quads, axis=1)
        scores = []
        for g in range(3):
            proj = jnp.dot(
                lhs_ref[g * 8 * FEAT : (g + 1) * 8 * FEAT], rhs, preferred_element_type=jnp.float32
            )
            proj = proj.reshape(FEAT, 8, 2 * COLS)
            distance = jnp.sum(proj * proj, axis=0)
            prior = prior_ref[g]
            scores.append(jnp.concatenate([prior, prior], axis=1) - 0.5 * distance)
        top = jnp.maximum(jnp.maximum(scores[0], scores[1]), scores[2])
        top = jnp.maximum(top, pltpu.roll(top, 4, 0))
        powers = [jnp.exp(s - top) for s in scores]
        total = powers[0] + powers[1] + powers[2]
        total = total + pltpu.roll(total, 4, 0)
        inverse = 1.0 / total
        for g in range(3):
            r = powers[g] * inverse
            left, right = r[:, :COLS], r[:, COLS:]
            for h in range(2):
                tile = jnp.concatenate(
                    [left[4 * h : 4 * h + 4], right[4 * h : 4 * h + 4]], axis=0
                )
                resp_ref[2 * g + h, z] = tile
                cnt_ref[2 * g + h] += tile

    def moment(z):
        features, weighted = [], []
        tiles = [resp_ref[k, z] for k in range(COMP)]
        for i in range(8):
            f = feats[i, z]
            f32 = f.astype(jnp.float32)
            features.append(jnp.concatenate([f, one_tile], axis=0))
            weighted.append(
                jnp.concatenate(
                    [(tiles[k][i : i + 1] * f32).astype(jnp.bfloat16) for k in range(COMP)],
                    axis=0,
                )
            )
        f_all = jnp.concatenate(features, axis=1)
        w_all = jnp.concatenate(weighted, axis=1)
        sec_ref[...] += lax.dot_general(
            w_all, f_all, (((1,), (1,)), ((), ())), preferred_element_type=jnp.float32
        )

    def expect_step(z, carry):
        expect(z)
        return carry

    def moment_step(z, carry):
        moment(z)
        return carry

    lax.fori_loop(0, PLANES, expect_step, 0, unroll=16)
    lax.fori_loop(0, PLANES, moment_step, 0, unroll=16)

    @pl.when(octet == pl.num_programs(0) - 1)
    def _():
        half = FEAT // 2
        row = lax.broadcasted_iota(jnp.int32, (half, 64), 0)
        lane = lax.broadcasted_iota(jnp.int32, (half, 64), 1)
        packed = []
        for k in range(COMP):
            upper = sec_ref[k * FEAT : k * FEAT + half]
            lower = sec_ref[k * FEAT + half : (k + 1) * FEAT]
            first = lower[:, FEAT : FEAT + 1]
            diagonal = jnp.sum(jnp.where(lane == row + half, lower, 0.0), axis=1, keepdims=True)
            block = jnp.where(lane < row, jnp.concatenate([lower[:, half:], lower[:, :half]], axis=1), upper)
            block = jnp.where(lane == FEAT + 1, first, block)
            block = jnp.where(lane == FEAT + 2, diagonal, block)
            packed.append(jnp.where(lane == FEAT + 3, jnp.sum(cnt_ref[k]), block))
        for m in range(3):
            both = jnp.concatenate(packed[2 * m : 2 * m + 2], axis=1)
            moment_ref[m * half : (m + 1) * half] = both


def prepare_kernel(weight_ref, mean_ref, factor_ref, lhs_ref, prior_ref, scale_ref):
    logits = weight_ref[...]
    top = jnp.max(logits, axis=1, keepdims=True)
    log_total = jnp.log(jnp.sum(jnp.exp(logits - top), axis=1, keepdims=True)) + top
    on_diagonal = lax.broadcasted_iota(jnp.int32, (FEAT, FEAT), 0) == lax.broadcasted_iota(
        jnp.int32, (FEAT, FEAT), 1
    )
    lane = lax.broadcasted_iota(jnp.int32, (FEAT, 256), 1)
    half = lax.broadcasted_iota(jnp.int32, (8, COLS), 0) < 4
    to_row = lax.broadcasted_iota(jnp.int32, (8 * FEAT, 8 * FEAT), 0)
    from_row = lax.broadcasted_iota(jnp.int32, (8 * FEAT, 8 * FEAT), 1)
    wanted = (to_row & 7) * FEAT + (to_row >> 3)
    order = jnp.where(wanted == from_row, 1.0, 0.0).astype(jnp.bfloat16)
    feature = lax.broadcasted_iota(jnp.int32, (FEAT, COLS), 0)
    for j, (oz, ox, oy) in enumerate(ORDER_TRIPLES):
        value = 1.0 / math.sqrt(TAP_NORMS[oz] * TAP_NORMS[ox] * TAP_NORMS[oy])
        scale = jnp.full((FEAT, COLS), value, jnp.float32) if j == 0 else jnp.where(lax.rem(feature, len(ORDER_TRIPLES)) == j, value, scale)
    scale_ref[...] = scale
    for g in range(3):
        rows, priors = [], []
        for h in range(2):
            k = 2 * g + h
            factor = factor_ref[k]
            log_diag = jnp.sum(jnp.where(on_diagonal, jnp.log(jnp.where(on_diagonal, factor, 1.0)), 0.0))
            prior = logits[:, k : k + 1] - log_total + log_diag - 0.5 * FEAT * math.log(2.0 * math.pi)
            priors.append(jnp.broadcast_to(prior, (8, COLS)))
            columns = factor.astype(jnp.bfloat16).astype(jnp.float32).T
            offset = jnp.sum(columns * mean_ref[k : k + 1], axis=1, keepdims=True)
            rest = -offset
            tail = jnp.zeros((FEAT, 256), jnp.float32)
            for t in range(3):
                term = rest.astype(jnp.bfloat16).astype(jnp.float32)
                tail = jnp.where(lane == 4 * FEAT + t, term, tail)
                rest = rest - term
            wide = jnp.concatenate([columns, jnp.zeros((FEAT, 256 - FEAT), jnp.float32)], axis=1)
            for x in range(4):
                moved = wide if x == 0 else pltpu.roll(wide, x * FEAT, 1)
                rows.append((moved + tail).astype(jnp.bfloat16))
        block = jnp.dot(order, jnp.concatenate(rows, axis=0), preferred_element_type=jnp.float32)
        lhs_ref[g * 8 * FEAT : (g + 1) * 8 * FEAT] = block[:, :DEEP].astype(jnp.bfloat16)
        prior_ref[g] = jnp.where(half, priors[0], priors[1])


def vmem_specs(count):
    return [pl.BlockSpec(memory_space=pltpu.VMEM)] * count


def prepare(log_weights, means, prec_factor):
    return pl.pallas_call(
        prepare_kernel,
        in_specs=vmem_specs(3),
        out_specs=vmem_specs(3),
        out_shape=[
            jax.ShapeDtypeStruct((COMP * FEAT * 4, DEEP), jnp.bfloat16),
            jax.ShapeDtypeStruct((3, 8, COLS), jnp.float32),
            jax.ShapeDtypeStruct((FEAT, COLS), jnp.float32),
        ],
        cost_estimate=pl.CostEstimate(flops=10**8, bytes_accessed=2 * 10**6, transcendentals=2 * 10**4),
        compiler_params=pltpu.CompilerParams(vmem_limit_bytes=8 * 2**20),
        name="prepare",
    )(log_weights.reshape(1, COMP), means, prec_factor)


def pick(block, column):
    lane = lax.broadcasted_iota(jnp.int32, block.shape, 1)
    return jnp.sum(jnp.where(lane == column, block, 0.0), axis=1, keepdims=True)


def finish_kernel(a_ref, b_ref, c_ref, d_ref, weight_ref, mean_ref, cov_ref):
    half = FEAT // 2
    row = lax.broadcasted_iota(jnp.int32, (FEAT, FEAT), 0)
    col = lax.broadcasted_iota(jnp.int32, (FEAT, FEAT), 1)
    stored = ((row < half) & (col >= row)) | ((row >= half) & (col >= half) & (col < row))
    lane = lax.broadcasted_iota(jnp.int32, (1, COMP), 1)
    counts = jnp.zeros((1, COMP), jnp.float32)
    for k in range(COMP):
        at = slice(k // 2 * half, (k // 2 + 1) * half)
        both = (a_ref[at] + b_ref[at]) + (c_ref[at] + d_ref[at])
        block = both if k % 2 == 0 else pltpu.roll(both, 64, 1)
        upper = block[:, :FEAT]
        lower = pltpu.roll(block, half, 1)[:, :FEAT]
        second = jnp.concatenate([upper, lower], axis=0)
        second = jnp.where(stored, second, second.T)
        diagonal = pick(block, FEAT + 2)
        diagonal = jnp.concatenate([diagonal, diagonal], axis=0)
        second = jnp.where((row == col) & (row >= half), diagonal, second)
        first = jnp.concatenate([pick(block, FEAT), pick(block, FEAT + 1)], axis=0)
        count = pick(block, FEAT + 3)[:1]
        column = first / count
        across = jnp.sum(jnp.where(row == col, column, 0.0), axis=0, keepdims=True)
        cov_ref[k] = second / count - column * across
        mean_ref[k : k + 1] = across
        counts = jnp.where(lane == k, count, counts)
    weight_ref[...] = counts / jnp.sum(counts, axis=1, keepdims=True)


def finish(*parts):
    new_weights, new_means, new_cov = pl.pallas_call(
        finish_kernel,
        in_specs=vmem_specs(4),
        out_specs=vmem_specs(3),
        out_shape=[
            jax.ShapeDtypeStruct((1, COMP), jnp.float32),
            jax.ShapeDtypeStruct((COMP, FEAT), jnp.float32),
            jax.ShapeDtypeStruct((COMP, FEAT, FEAT), jnp.float32),
        ],
        compiler_params=pltpu.CompilerParams(vmem_limit_bytes=8 * 2**20),
        name="finish",
    )(*parts)
    return new_weights.reshape(COMP), new_means, new_cov


def local_step(pieces, lhs, prior, scale):
    filt = jnp.asarray(filter_matrix(), jnp.bfloat16)
    full = lambda *shape: pl.BlockSpec(shape, lambda o: (0,) * len(shape))
    return pl.pallas_call(
        kernel,
        grid=(ROWS // 8,),
        in_specs=[
            *[full(*piece.shape) for piece in pieces],
            pl.BlockSpec(memory_space=pltpu.HBM),
            full(*scale.shape),
            full(*lhs.shape),
            full(*prior.shape),
        ],
        out_specs=[
            pl.BlockSpec((COMP, PLANES, 8, COLS), lambda o: (0, 0, o, 0)),
            full(3 * FEAT // 2, 128),
        ],
        out_shape=[
            jax.ShapeDtypeStruct((COMP, PLANES, ROWS, COLS), jnp.float32),
            jax.ShapeDtypeStruct((3 * FEAT // 2, 128), jnp.float32),
        ],
        scratch_shapes=[
            pltpu.VMEM((len(SHIFTS), ROWS + 2 * MARGIN, PLANES, COLS), jnp.bfloat16),
            pltpu.VMEM((8, PLANES, FEAT, COLS), jnp.bfloat16),
            pltpu.VMEM((COMP * FEAT, FEAT + 16), jnp.float32),
            pltpu.VMEM((COMP, 8, COLS), jnp.float32),
            pltpu.VMEM(filt.shape, filt.dtype),
            pltpu.SemaphoreType.DMA,
        ],
        compiler_params=pltpu.CompilerParams(
            dimension_semantics=("arbitrary",), vmem_limit_bytes=32 * 2**20
        ),
        name="mixture_step",
    )(*pieces, filt, scale, lhs, prior)


def pack_kernel(rows_ref, head_ref, tail_ref):
    for n in range(ROWS // 8):
        group = [rows_ref[8 * n + m] for m in range(8)]
        head_ref[n] = jnp.concatenate([row[:, :MARGIN] for row in group], axis=1)
        tail_ref[n] = jnp.concatenate([row[:, COLS - MARGIN :] for row in group], axis=1)


def pack(rows):
    shape = jax.ShapeDtypeStruct((ROWS // 8, PLANES, COLS), jnp.bfloat16)
    return pl.pallas_call(
        pack_kernel,
        in_specs=vmem_specs(1),
        out_specs=vmem_specs(2),
        out_shape=[shape, shape],
        compiler_params=pltpu.CompilerParams(vmem_limit_bytes=8 * 2**20),
        name="pack",
    )(rows)


def neighbours(to_next, to_previous, axis):
    ends = lax.axis_size(axis) - 1
    before = lax.ppermute(to_next, axis, [(i, i + 1) for i in range(ends)])
    after = lax.ppermute(to_previous, axis, [(i + 1, i) for i in range(ends)])
    return before, after


def wide_perm(move):
    perm = []
    for i in range(32):
        x, y, c = move(i // 8, (i // 2) % 4, i % 2)
        perm.append((i, (x * 4 + y) * 2 + c))
    return perm


def device_sum(part):
    got = []
    for c in range(2):
        for d in range(4):
            if c + d:
                perm = [(4 * w + n, 4 * (w ^ c) + (n + d) % 4) for w in range(32) for n in range(4)]
                got.append(lax.ppermute(part, ("wide", "narrow"), perm))
    part = (part + got[0]) + (got[1] + got[2]) + ((got[3] + got[4]) + (got[5] + got[6]))
    for axis in range(2):
        got = []
        for d in (1, 2, 3):
            if axis == 0:
                perm = wide_perm(lambda x, y, c: (x, (y + d) % 4, c))
            else:
                perm = wide_perm(lambda x, y, c: ((x + d) % 4, y, c))
            got.append(lax.ppermute(part, "wide", perm))
        if axis == 0:
            part = (part + got[0]) + (got[1] + got[2])
    return [part] + got


def shards(volume, log_weights, means, prec_factor):
    rows = jnp.transpose(volume, (1, 0, 2))
    head, tail = pack(rows)
    left, right = neighbours(tail, head, "narrow")
    lhs, prior, scale = prepare(log_weights, means, prec_factor)
    bottom = jnp.concatenate([rows[ROWS - MARGIN :], left[6:], right[6:]], axis=0)
    top = jnp.concatenate([rows[:MARGIN], left[:2], right[:2]], axis=0)
    before, after = neighbours(bottom, top, "wide")
    responsibility, moments = local_step((before, rows, after, left, right), lhs, prior, scale)
    return (responsibility,) + finish(*device_sum(moments))


def solution(mesh):
    in_specs = (P(None, "wide", "narrow"), P(), P(), P())
    out_specs = (P(None, None, "wide", "narrow"), P(), P(), P())
    return jax.shard_map(shards, mesh=mesh, in_specs=in_specs, out_specs=out_specs, check_vma=False)
```
